32 devices in a mesh: page: 8 (over z, x), tok: 4 (over y, core).
Axes of the slice: x: 2, y: 2, z: 4, core: 2. Of those that a mesh axis runs over, the one named last changes fastest.
Arguments:
- tile_tokens: bfloat16 [8, 4096, 1024], P('page', 'tok'), may hold values from -6 to 6
- page_lengths: int32 [8], P('page'), may hold values from 1 to 4096, as said below
- occupancy: int32 [8, 32], P('page', 'tok'), may hold values 0 or 1
- block_mix: bfloat16 [32, 128, 128], P('tok'), may hold values from -0.5 to 0.5
- stride_mix: bfloat16 [128, 32, 32], P('tok'), may hold values from -1 to 1
- w_gate_up: bfloat16 [2, 1024, 2048], P(None, None, ('page', 'tok')), may hold values from -0.1875 to 0.1875
- w_down: bfloat16 [2048, 1024], P(None, ('page', 'tok')), may hold values from -0.125 to 0.125
Outputs:
- packed_lanes: bfloat16 [4, 8192, 1024], P('tok', 'page')
The draws below stay inside these ranges and needn't reach their ends.
Inputs may be any that keep to these rules, and one draw needn't show every extreme that they name: `page_lengths`: some page has exactly 4096 used tokens in every draw; page 0 has fewer than 1024 used tokens in every draw.
All inputs are finite; a program needn't handle non-finite values. No bound on the sum of `occupancy` on one device may be relied on, other than what follows from the above.
Results may differ from the reference program's by a relative error of at most 0.012.
Values may be sent and summed in bfloat16 or wider, within the bound.
No kernel may reach another device: no remote copies, remote signals or barrier semaphores. Data moves between devices by JAX's collectives and lax.ppermute only.
A program may use at most 64 MiB of HBM per device.

```python
import jax
import jax.numpy as jnp
from jax import lax

D = 1024
FF = 2048
BLK = 128
NB = 32
PAGE_LEN = 4096
N_PAGE = 8
N_TOK = 4


def draw_page_lengths(key, part):
    full_len = NB * BLK
    lane_rows = full_len // N_TOK
    key_one, key_two, key_top, key_head = jax.random.split(key, 4)
    draw_one = jax.random.randint(key_one, (N_PAGE,), 1, full_len + 1)
    draw_two = jax.random.randint(key_two, (N_PAGE,), 1, full_len + 1)
    lengths = jnp.minimum(draw_one, draw_two)
    head_len = jax.random.randint(key_head, (), 1, lane_rows)
    longest = jax.random.randint(key_top, (), 1, N_PAGE)
    page_ids = jnp.arange(N_PAGE)
    lengths = jnp.where(page_ids == 0, head_len, lengths)
    return jnp.where(page_ids == longest, full_len, lengths).astype(jnp.int32)


def touch_ends(values, key, least, high):
    place = [jax.random.randint(jax.random.fold_in(key, axis), (), 0, length) for axis, length in enumerate(values.shape)]
    widest = values.shape.index(max(values.shape))
    neighbour = place[:widest] + [(place[widest] + 1) % values.shape[widest]] + place[widest + 1:]
    return values.at[tuple(place)].set(least).at[tuple(neighbour)].set(high)


def steps_of(own_key, extent, shards, least, high):
    def one(dim, parts):
        draws = jax.random.uniform(jax.random.fold_in(jax.random.fold_in(own_key, 6), dim), (parts,), jnp.float32, least / len(shards), high / len(shards))
        return jnp.repeat(jnp.exp(draws), extent[dim] // parts).reshape((-1,) + (1,) * (len(extent) - dim - 1))

    loudness = one(*shards[0])
    for cut in shards[1:]:
        loudness = loudness * one(*cut)
    return loudness


def scatter_about(rng, extent, scale, reach, cuts=(), kind=jnp.bfloat16):
    gain = steps_of(rng, extent, cuts, -0.22, 0.18) if cuts else 1.0
    drawn = jax.random.normal(rng, extent, jnp.float32) * scale * gain
    return jnp.minimum(jnp.maximum(drawn, -reach), reach).astype(kind)


def setup_inputs(seed: int = 0) -> dict:
    arg_keys = jax.random.split(jax.random.key(seed), 8)
    return {
        "tile_tokens": scatter_about(arg_keys[0], (N_PAGE, PAGE_LEN, D), 1.0, 6.0, ((0, 8), (1, 4))),
        "page_lengths": draw_page_lengths(jax.random.fold_in(arg_keys[7], 71), 0),
        "occupancy": touch_ends((jax.random.randint(arg_keys[2], (N_PAGE, NB), 0, 4) < 3).astype(jnp.int32), jax.random.fold_in(arg_keys[2], 1), 0, 1),
        "block_mix": scatter_about(arg_keys[3], (NB, BLK, BLK), BLK ** -0.5, 0.5, ((0, 4),)),
        "stride_mix": scatter_about(arg_keys[4], (BLK, NB, NB), NB ** -0.5, 1.0, ((0, 4),)),
        "w_gate_up": scatter_about(arg_keys[5], (2, D, FF), D ** -0.5, 0.1875, ((2, 32),)),
        "w_down": scatter_about(arg_keys[6], (FF, D), FF ** -0.5, 0.125, ((1, 32),)),
    }


epsilon = 1e-05

def rms_round(values):
    scale = lax.rsqrt(lax.optimization_barrier(jnp.mean(values * values, axis=-1, keepdims=True)) + epsilon)
    return (values * scale).astype(jnp.bfloat16)

def one_page(inputs, block_mix, stride_mix, w_gate_up, w_down):
    tile_rows, length, occ_row = inputs
    page_len = NB * BLK
    positions = jnp.arange(page_len, dtype=jnp.int32)
    live_mask = (positions < length) & (jnp.repeat(occ_row, BLK) > 0)
    masked = jnp.where(live_mask[:, None], tile_rows.astype(jnp.float32), 0.0)
    normed = rms_round(masked).reshape(NB, BLK, D)
    first = jnp.einsum('bji,bic->bjc', block_mix.astype(jnp.float32), normed.astype(jnp.float32)).astype(jnp.bfloat16)
    second = jnp.einsum('jkb,bjc->jkc', stride_mix.astype(jnp.float32), first.astype(jnp.float32))
    mixed = (masked + second.reshape(page_len, D)).astype(jnp.bfloat16)
    mixed_float = mixed.astype(jnp.float32)
    normed_two = rms_round(mixed_float)
    gate_vals = jnp.dot(normed_two, w_gate_up[0], preferred_element_type=jnp.float32)
    up_vals = jnp.dot(normed_two, w_gate_up[1], preferred_element_type=jnp.float32)
    hidden = (jax.nn.silu(gate_vals) * up_vals).astype(jnp.bfloat16)
    down_vals = jnp.dot(hidden, w_down, preferred_element_type=jnp.float32)
    return (mixed_float + down_vals).astype(jnp.bfloat16)

def reference(tile_tokens, page_lengths, occupancy, block_mix, stride_mix, w_gate_up, w_down):
    layer_out = lax.map(lambda inputs: one_page(inputs, block_mix, stride_mix, w_gate_up, w_down), (tile_tokens, page_lengths, occupancy))
    lane_count = N_TOK
    row_count = NB * BLK // lane_count
    lane_index = jnp.arange(lane_count, dtype=jnp.int32)
    kept = jnp.clip(page_lengths[:, None] - lane_index[None, :] * row_count, 0, row_count).astype(jnp.int32)
    offset = (jnp.cumsum(kept, axis=0) - kept).astype(jnp.int32)
    rows_in = jnp.arange(row_count, dtype=jnp.int32)
    total_rows = N_PAGE * row_count
    target = offset[:, :, None] + rows_in[None, None, :]
    target = jnp.where(rows_in[None, None, :] < kept[:, :, None], target, total_rows).astype(jnp.int32)
    pieces = layer_out.reshape(N_PAGE, lane_count, row_count, D)

    def one_lane(lane):
        dest = lax.dynamic_index_in_dim(target, lane, 1, keepdims=False).reshape(-1)
        rows_here = lax.dynamic_index_in_dim(pieces, lane, 1, keepdims=False).reshape(-1, D)
        empty = jnp.zeros((total_rows, D), jnp.bfloat16)
        return empty.at[dest].set(rows_here, mode='drop')
    return lax.map(one_lane, lane_index)
```

```python
import functools

import jax
import jax.numpy as jnp
from jax import lax
from jax.experimental import pallas as pl
from jax.experimental.pallas import tpu as pltpu
from jax.sharding import PartitionSpec as P

epsilon = 1e-05


def entering(value, axis, join, neutral):
    count, mine = (lax.axis_size(axis), lax.axis_index(axis))
    pieces = lax.all_gather(value, axis)
    so_far = jnp.full_like(value, 0) + jnp.asarray(neutral, value.dtype)

    def hop(position, so_far):
        longer = join(so_far, pieces[position])
        return jnp.where(position < mine, longer, so_far)

    return lax.fori_loop(0, count - 1, hop, so_far)


def from_behind(value, axis, by):
    length = lax.axis_size(axis)
    pairs = [(i, i + by) for i in range(length) if 0 <= i + by < length]
    return lax.ppermute(value, axis, pairs)


def rms_round(values):
    scale = lax.rsqrt(jnp.mean(values * values, axis=-1, keepdims=True) + epsilon)
    return (values * scale).astype(jnp.bfloat16)


def add_counts(earlier, later):
    return earlier + later


def channel_mlp(mixed, w_gate_up, w_down):
    mixed_float = mixed.astype(jnp.float32)
    normed_two = rms_round(mixed_float)
    shard_part = lax.all_gather(w_gate_up, ("page", "tok"), axis=2, tiled=True)
    gate_vals = jnp.dot(normed_two, shard_part[0], preferred_element_type=jnp.float32)
    up_vals = jnp.dot(normed_two, shard_part[1], preferred_element_type=jnp.float32)
    hidden = (jax.nn.silu(gate_vals) * up_vals).astype(jnp.bfloat16)
    down_vals = jnp.dot(
        hidden,
        lax.all_gather(w_down, ("page", "tok"), axis=1, tiled=True),
        preferred_element_type=jnp.float32,
    )
    return (mixed_float + down_vals).astype(jnp.bfloat16)


def lane_relay(row_data, length, lane_index):
    row_count = row_data.shape[0]
    page_here = lax.axis_index("page")
    live_rows = jnp.clip(length - lane_index * row_count, 0, row_count)
    before = entering(live_rows.reshape(1), "page", add_counts, jnp.zeros((1,), jnp.int32))[0]
    distance = page_here * row_count - before
    in_shift = distance % row_count
    hop_count = distance // row_count
    row_ids = jnp.arange(row_count, dtype=jnp.int32)
    live_flag = row_ids < live_rows
    kept_data = jnp.where(live_flag[:, None], row_data, jnp.zeros_like(row_data))
    kept_tags = jnp.where(live_flag, hop_count + 1, 0).astype(jnp.int32)
    zero_data = jnp.zeros_like(row_data)
    zero_tags = jnp.zeros_like(kept_tags)
    here_data = lax.dynamic_slice_in_dim(
        jnp.concatenate([kept_data, zero_data], 0), in_shift, row_count, 0
    )
    here_tags = lax.dynamic_slice_in_dim(
        jnp.concatenate([kept_tags, zero_tags], 0), in_shift, row_count, 0
    )
    spill_data = lax.dynamic_slice_in_dim(
        jnp.concatenate([zero_data, kept_data], 0), in_shift, row_count, 0
    )
    spill_tags = lax.dynamic_slice_in_dim(
        jnp.concatenate([zero_tags, kept_tags], 0), in_shift, row_count, 0
    )
    got_data, got_tags = from_behind((spill_data, spill_tags), "page", -1)
    arrived = got_tags > 0
    cur_data = jnp.where(arrived[:, None], got_data, here_data)
    cur_tags = jnp.where(arrived, got_tags, here_tags)
    for bit_pos in range((lax.axis_size("page") - 1).bit_length()):
        stride_len = 1 << bit_pos
        present = cur_tags > 0
        moving = present & ((cur_tags - 1) // stride_len % 2 == 1)
        staying = present & jnp.logical_not(moving)
        out_data = jnp.where(moving[:, None], cur_data, jnp.zeros_like(cur_data))
        out_tags = jnp.where(moving, cur_tags, 0)
        got_data, got_tags = from_behind((out_data, out_tags), "page", -stride_len)
        arrived = got_tags > 0
        kept_now = jnp.where(staying[:, None], cur_data, jnp.zeros_like(cur_data))
        cur_data = jnp.where(arrived[:, None], got_data, kept_now)
        cur_tags = jnp.where(arrived, got_tags, jnp.where(staying, cur_tags, 0))
    return cur_data


def per_device(tile_tokens, page_lengths, occupancy, block_mix, stride_mix, w_gate_up, w_down):
    lane_index = lax.axis_index("tok")
    row_count = tile_tokens.shape[1]
    feat_width = tile_tokens.shape[2]
    blocks_here = block_mix.shape[0]
    blk_size = block_mix.shape[1]
    length = page_lengths[0]
    positions = lane_index * row_count + jnp.arange(row_count, dtype=jnp.int32)
    live_mask = (positions < length) & (jnp.repeat(occupancy[0], blk_size) > 0)
    masked = jnp.where(live_mask[:, None], tile_tokens[0].astype(jnp.float32), 0.0)
    normed = rms_round(masked).reshape(blocks_here, blk_size, feat_width)
    first = jnp.einsum(
        "bji,bic->bjc", block_mix, normed, preferred_element_type=jnp.float32
    ).astype(jnp.bfloat16)
    second = jnp.einsum(
        "jkb,bjc->jkc",
        stride_mix,
        lax.all_to_all(first, "tok", split_axis=1, concat_axis=0, tiled=True),
        preferred_element_type=jnp.float32,
    )
    mixed = (masked + second.reshape(row_count, feat_width)).astype(jnp.bfloat16)
    layer_out = channel_mlp(mixed, w_gate_up, w_down)
    packed = lane_relay(layer_out, length, lane_index)
    return packed.reshape(1, row_count, feat_width)


SMEM = pl.BlockSpec(memory_space=pltpu.SMEM)
VMEM = pl.BlockSpec(memory_space=pltpu.VMEM)
ANY = pl.BlockSpec(memory_space=pl.ANY)
VMEM_LIMIT = 56 * 1024 * 1024


def params():
    return pltpu.CompilerParams(vmem_limit_bytes=VMEM_LIMIT)


def live_rows(start, rows, length, occupied):
    ids = start + lax.broadcasted_iota(jnp.int32, (rows, 1), 0)
    return (ids < length) & (occupied > 0)


def first_kernel(ids_ref, length_ref, occ_ref, tile_ref, mix_ref, *out_refs):
    block = pl.program_id(0)
    blk_size = tile_ref.shape[1]
    rows_here = pl.num_programs(0) * blk_size
    start = ids_ref[1] * rows_here + block * blk_size
    live = live_rows(start, blk_size, length_ref[0], occ_ref[0, block])
    masked = jnp.where(live, tile_ref[0].astype(jnp.float32), 0.0)
    normed = rms_round(masked)
    first = jnp.dot(mix_ref[0], normed, preferred_element_type=jnp.float32).astype(jnp.bfloat16)
    parts, _, share, width = out_refs[0].shape
    for half, out_ref in enumerate(out_refs):
        for part in range(parts):
            out_ref[part, 0] = first[part * share:(part + 1) * share, half * width:(half + 1) * width]


def first_factor(ids, length, occupancy, tile_tokens, block_mix, parts, halves):
    blocks, blk_size, _ = block_mix.shape
    feat_width = tile_tokens.shape[2]
    share, width = blk_size // parts, feat_width // halves
    return pl.pallas_call(
        first_kernel,
        grid=(blocks,),
        in_specs=[
            SMEM,
            SMEM,
            SMEM,
            pl.BlockSpec((1, blk_size, feat_width), lambda b: (0, b, 0)),
            pl.BlockSpec((1, blk_size, blk_size), lambda b: (b, 0, 0)),
        ],
        out_specs=[pl.BlockSpec((parts, 1, share, width), lambda b: (0, b, 0, 0))] * halves,
        out_shape=[jax.ShapeDtypeStruct((parts, blocks, share, width), jnp.bfloat16)] * halves,
        compiler_params=params(),
        name="first_factor",
    )(ids, length, occupancy, tile_tokens, block_mix)


GROUP = 16
SUB = 8


def spread_kernel(stride_ref, out_ref):
    spots, outs, ins = stride_ref.shape
    rows, cols = GROUP * outs, GROUP * ins
    picks = lax.broadcasted_iota(jnp.int32, (ins, cols), 1) // GROUP
    picks = picks == lax.broadcasted_iota(jnp.int32, (ins, cols), 0)
    picks = picks.astype(jnp.float32).astype(jnp.bfloat16)
    spot_row = lax.broadcasted_iota(jnp.int32, (rows, cols), 0) // outs
    spot_col = lax.broadcasted_iota(jnp.int32, (rows, cols), 1) % GROUP
    for group in range(spots // GROUP):
        flat = stride_ref[group * GROUP:(group + 1) * GROUP].reshape(rows, ins)
        wide = jnp.dot(flat, picks, preferred_element_type=jnp.float32)
        out_ref[group] = jnp.where(spot_row == spot_col, wide, 0.0).astype(jnp.bfloat16)


def spread_stride(stride_mix):
    spots, outs, ins = stride_mix.shape
    return pl.pallas_call(
        spread_kernel,
        in_specs=[VMEM],
        out_specs=VMEM,
        out_shape=jax.ShapeDtypeStruct((spots // GROUP, GROUP * outs, GROUP * ins), jnp.bfloat16),
        compiler_params=params(),
        name="spread_stride",
    )(stride_mix)


def kept_of(length, lane, rows):
    return jnp.clip(length - lane * rows, 0, rows)


def offset_of(lengths_ref, page, lane, rows):
    total = jnp.int32(0)
    for earlier in range(lengths_ref.shape[0]):
        total += jnp.where(earlier < page, kept_of(lengths_ref[earlier], lane, rows), 0)
    return total


def second_kernel(ids_ref, lengths_ref, occ_ref, spread_ref, first_ref, tile_ref, *refs):
    out_refs, twice_ref = refs[:-1], refs[-1]
    rows, width = tile_ref.shape[1:]
    page, lane = ids_ref[0], ids_ref[1]
    length = lengths_ref[page]
    groups, group_rows, depth = spread_ref.shape
    blocks = occ_ref.shape[1]
    blk_size = rows // blocks
    for group in range(groups):
        values = first_ref[:, group * GROUP:(group + 1) * GROUP, :].reshape(depth, width)
        second = jnp.dot(spread_ref[group], values, preferred_element_type=jnp.float32)
        for part in range(group_rows // blk_size):
            at = group * group_rows + part * blk_size
            live = live_rows(lane * rows + at, blk_size, length, occ_ref[0, at // blk_size])
            masked = jnp.where(live, tile_ref[0, at:at + blk_size, :].astype(jnp.float32), 0.0)
            mixed = masked + second[part * blk_size:(part + 1) * blk_size]
            mixed = mixed.astype(jnp.bfloat16).astype(jnp.float32)
            twice_ref[at:at + blk_size, :] = mixed
            twice_ref[rows + at:rows + at + blk_size, :] = mixed
    shift = offset_of(lengths_ref, page, lane, rows) % rows
    start = rows - shift
    extra = start % SUB
    base = pl.multiple_of(start - extra, SUB)
    tall = twice_ref[pl.ds(base, rows + SUB), :].reshape(rows // SUB + 1, SUB, width)
    tall = pltpu.roll(tall, (SUB - extra) % SUB, 1)
    inside = lax.broadcasted_iota(jnp.int32, (1, SUB, 1), 1) + extra < SUB
    turned = jnp.where(inside, tall[:-1], tall[1:]).reshape(rows, width).astype(jnp.bfloat16)
    for part, out_ref in enumerate(out_refs):
        span = out_ref.shape[1]
        out_ref[...] = turned[:, part * span:(part + 1) * span]


def second_factor(half, pieces, ids, lengths, occupancy, spread, first, tile_tokens):
    rows = tile_tokens.shape[1]
    width = first.shape[2]
    return pl.pallas_call(
        second_kernel,
        grid=(1,),
        in_specs=[
            SMEM,
            SMEM,
            SMEM,
            VMEM,
            VMEM,
            pl.BlockSpec((1, rows, width), lambda i: (0, 0, half)),
        ],
        out_specs=[VMEM] * pieces,
        out_shape=[jax.ShapeDtypeStruct((rows, width // pieces), jnp.bfloat16)] * pieces,
        scratch_shapes=[pltpu.VMEM((2 * rows + SUB, width), jnp.float32)],
        compiler_params=params(),
        name="second_factor",
    )(ids, lengths, occupancy, spread, first, tile_tokens)


def parity_kernel(ids_ref, lengths_ref, own_ref, got_ref, out_ref):
    rows = own_ref.shape[0]
    page, lane = ids_ref[0], ids_ref[1]
    offset = offset_of(lengths_ref, page, lane, rows)
    kept = kept_of(lengths_ref[page], lane, rows)
    slot = lax.broadcasted_iota(jnp.int32, (rows, 1), 0)
    base = offset // rows
    shift = offset % rows
    late = slot < shift
    row = jnp.where(late, slot + rows, slot) - shift
    target = jnp.where(late, base + 1, base)
    mine = (row < kept) & (target % 2 == page % 2)
    out_ref[...] = jnp.where(mine, own_ref[...], got_ref[...])


def join_parity(ids, lengths, own, got):
    return pl.pallas_call(
        parity_kernel,
        in_specs=[SMEM, SMEM, VMEM, VMEM],
        out_specs=VMEM,
        out_shape=jax.ShapeDtypeStruct(own.shape, own.dtype),
        compiler_params=params(),
        name="join_parity",
    )(ids, lengths, own, got)


def forward_kernel(ids_ref, lengths_ref, own_ref, one_ref, two_ref, out_ref):
    rows = own_ref.shape[0]
    page, lane = ids_ref[0], ids_ref[1]
    level = page // 2
    slot = (page % 2) * rows + lax.broadcasted_iota(jnp.int32, (rows, 1), 0)
    after_one = offset_of(lengths_ref, 2 * level + 2, lane, rows)
    after_two = offset_of(lengths_ref, 2 * level + 4, lane, rows)
    value = jnp.where(slot < after_two, one_ref[...], two_ref[...])
    out_ref[...] = jnp.where(slot < after_one, own_ref[...], value)


def forward_merge(ids, lengths, own, one, two):
    return pl.pallas_call(
        forward_kernel,
        in_specs=[SMEM, SMEM, VMEM, VMEM, VMEM],
        out_specs=VMEM,
        out_shape=jax.ShapeDtypeStruct(own.shape, own.dtype),
        compiler_params=params(),
        name="forward_merge",
    )(ids, lengths, own, one, two)


def mlp_kernel(pieces, ids_ref, lengths_ref, *refs):
    sources, refs = refs[:4 * pieces], refs[4 * pieces:]
    weights, out_ref, refs = refs[:4], refs[4], refs[5:]
    gate_ref, up_ref, low_ref, high_ref, sems = refs
    step = pl.program_id(0)
    rows = out_ref.shape[1]
    page, lane = ids_ref[0], ids_ref[1]
    core = lane % 2

    @pl.when(step == 0)
    def _():
        copies = []
        for side, main_ref, down_ref in ((0, gate_ref, low_ref), (1, up_ref, high_ref)):
            for other in range(2):
                src = weights[2 * side + other]
                where = core if other == 0 else 1 - core
                half = src.shape[0]
                wide = main_ref.shape[0] // (2 * half)
                thin = down_ref.shape[0] // (2 * half)
                main = main_ref.reshape(half, 2, wide, main_ref.shape[1])
                down = down_ref.reshape(half, 2, thin, down_ref.shape[1])
                copies.append(pltpu.make_async_copy(src.at[:, :wide], main.at[:, where], sems.at[4 * side + 2 * other]))
                copies.append(pltpu.make_async_copy(src.at[:, wide:], down.at[:, where], sems.at[4 * side + 2 * other + 1]))
        for copy in copies:
            copy.start()
        for copy in copies:
            copy.wait()

    lane_rows = rows * pl.num_programs(0)
    slot = page * lane_rows + step * rows + lax.broadcasted_iota(jnp.int32, (rows, 1), 0)
    level = page // 2
    ends = [offset_of(lengths_ref, 2 * (level + ahead), lane, lane_rows) for ahead in (1, 2)]
    total = offset_of(lengths_ref, lengths_ref.shape[0], lane, lane_rows)
    last_level = level == 0
    chunks = []
    for piece in range(pieces):
        own, one, two, last = (ref[...].astype(jnp.float32) for ref in sources[4 * piece:4 * piece + 4])
        far = jnp.where(last_level, last, jnp.where(slot < ends[1], one, two))
        value = jnp.where(slot < ends[0], own, far)
        chunks.append(jnp.where(slot < total, value, 0.0))
    mixed = jnp.concatenate(chunks, axis=1)
    normed = rms_round(mixed)
    contract = (((1,), (1,)), ((), ()))
    depth = low_ref.shape[1]
    count = 4
    span = gate_ref.shape[0] // count
    result = mixed
    for part in range(count):
        at = part * span
        gate = lax.dot_general(normed, gate_ref[at:at + span, :], contract, preferred_element_type=jnp.float32)
        up = lax.dot_general(normed, up_ref[at:at + span, :], contract, preferred_element_type=jnp.float32)
        hidden = (gate / (1.0 + jnp.exp(-gate)) * up).astype(jnp.bfloat16)
        down_ref = low_ref if at < depth else high_ref
        inner = at % depth
        result += lax.dot_general(hidden, down_ref[:, inner:inner + span], contract, preferred_element_type=jnp.float32)
    out_ref[0] = result.astype(out_ref.dtype)


def packed_mlp(ids, lengths, sources, weights, feat_width, hidden_width):
    rows, span = sources[0].shape
    pieces = len(sources) // 4
    steps = 4
    block = rows // steps
    depth = weights[0].shape[2]
    return pl.pallas_call(
        functools.partial(mlp_kernel, pieces),
        grid=(steps,),
        in_specs=[SMEM, SMEM] + [pl.BlockSpec((block, span), lambda i: (i, 0))] * len(sources) + [ANY] * 4,
        out_specs=pl.BlockSpec((1, block, feat_width), lambda i: (0, i, 0)),
        out_shape=jax.ShapeDtypeStruct((1, rows, feat_width), jnp.bfloat16),
        scratch_shapes=[
            pltpu.VMEM((hidden_width, feat_width), jnp.bfloat16),
            pltpu.VMEM((hidden_width, feat_width), jnp.bfloat16),
            pltpu.VMEM((feat_width, depth), jnp.bfloat16),
            pltpu.VMEM((feat_width, depth), jnp.bfloat16),
            pltpu.SemaphoreType.DMA((8,)),
        ],
        compiler_params=params(),
        name="packed_mlp",
    )(ids, lengths, *sources, *weights)


def swap(value, axis, bit):
    return lax.ppermute(value, axis, [(i, i ^ bit) for i in range(lax.axis_size(axis))])


def both_orders(value, got, bit, place):
    low = jnp.stack([value, got], place)
    high = jnp.stack([got, value], place)
    return jnp.where(bit == 0, low, high)


def gather_weights(w_gate_up, w_down):
    page, tok = lax.axis_index("page"), lax.axis_index("tok")
    pages = lax.axis_size("page")
    gate_up = jnp.swapaxes(w_gate_up, 1, 2)
    down = jnp.swapaxes(w_down, 0, 1)
    depth = gate_up.shape[2]
    own = jnp.concatenate([gate_up[0], down[:, :depth], gate_up[1], down[:, depth:]], 0)
    up_pairs = [(i, i + 2) for i in range(pages - 2)]
    down_pairs = [(i + 2, i) for i in range(pages - 2)]
    below, above = [own], [own]
    for _ in range(pages // 2 - 1):
        below.append(lax.ppermute(below[-1], "page", up_pairs))
        above.append(lax.ppermute(above[-1], "page", down_pairs))
    line = jnp.stack(below[:0:-1] + [own] + above[1:], 0)
    level = page // 2
    column = lax.dynamic_slice_in_dim(line, pages // 2 - 1 - level, pages // 2, 0)
    half = own.shape[0] // 2
    one, two = column[:, :half], column[:, half:]
    one = both_orders(one, swap(one, "page", 1), page % 2, 1)
    two = both_orders(two, swap(two, "tok", 2), tok // 2, 1)
    one = both_orders(one, swap(one, "tok", 2), tok // 2, 2)
    two = both_orders(two, swap(two, "page", 1), page % 2, 1)
    one = one.reshape((-1,) + one.shape[3:])
    two = two.reshape((-1,) + two.shape[3:])
    return [one, swap(one, "tok", 1), two, swap(two, "tok", 1)]


def all_lengths(length):
    pages = lax.axis_size("page")
    lengths = jnp.where(jnp.arange(pages) == lax.axis_index("page"), length, 0)
    bit = 1
    while bit < pages:
        lengths = lengths + swap(lengths, "page", bit)
        bit *= 2
    return lengths


def packed_device(tile_tokens, page_lengths, occupancy, block_mix, stride_mix, w_gate_up, w_down):
    ids = jnp.stack([lax.axis_index("page"), lax.axis_index("tok")]).astype(jnp.int32)
    parts = lax.axis_size("tok")
    pages = lax.axis_size("page")
    feat_width = tile_tokens.shape[2]
    weights = gather_weights(w_gate_up, w_down)
    halves, pieces = 2, 2
    firsts = first_factor(ids, page_lengths, occupancy, tile_tokens, block_mix, parts, halves)
    lengths = all_lengths(page_lengths[0])
    spread = spread_stride(stride_mix)
    sources = []
    for half, first in enumerate(firsts):
        got = lax.all_to_all(first, "tok", split_axis=0, concat_axis=0)
        got = got.reshape((-1,) + got.shape[2:])
        turned = second_factor(half, pieces, ids, lengths, occupancy, spread, got, tile_tokens)
        for own in turned:
            current = join_parity(ids, lengths, own, swap(own, "page", 1))
            one = lax.ppermute(current, "page", [(i, i - 2) for i in range(pages // 2, pages)])
            two = lax.ppermute(current, "page", [(i, i - 4) for i in range(pages - 2, pages)])
            merged = forward_merge(ids, lengths, current, one, two)
            last = lax.ppermute(merged, "page", [(i, i - 2) for i in range(2, 4)])
            sources += [current, one, two, last]
    hidden_width = w_down.shape[0]
    return packed_mlp(ids, lengths, sources, weights, feat_width, hidden_width)


def solution(mesh):
    pages, parts = mesh.shape["page"], mesh.shape["tok"]
    return jax.shard_map(
        packed_device if (pages, parts) == (8, 4) else per_device,
        mesh=mesh,
        in_specs=(
            P("page", "tok", None),
            P("page"),
            P("page", "tok"),
            P("tok", None, None),
            P("tok", None, None),
            P(None, None, ("page", "tok")),
            P(None, ("page", "tok")),
        ),
        out_specs=P("tok", "page", None),
        check_vma=False,
    )
```

```python
import functools

import jax
import jax.numpy as jnp
from jax import lax
from jax.experimental import pallas as pl
from jax.experimental.pallas import tpu as pltpu
from jax.sharding import PartitionSpec as P

epsilon = 1e-05


def entering(value, axis, join, neutral):
    count, mine = (lax.axis_size(axis), lax.axis_index(axis))
    pieces = lax.all_gather(value, axis)
    so_far = jnp.full_like(value, 0) + jnp.asarray(neutral, value.dtype)

    def hop(position, so_far):
        longer = join(so_far, pieces[position])
        return jnp.where(position < mine, longer, so_far)

    return lax.fori_loop(0, count - 1, hop, so_far)


def from_behind(value, axis, by):
    length = lax.axis_size(axis)
    pairs = [(i, i + by) for i in range(length) if 0 <= i + by < length]
    return lax.ppermute(value, axis, pairs)


def rms_round(values):
    scale = lax.rsqrt(jnp.mean(values * values, axis=-1, keepdims=True) + epsilon)
    return (values * scale).astype(jnp.bfloat16)


def add_counts(earlier, later):
    return earlier + later


def channel_mlp(mixed, w_gate_up, w_down):
    mixed_float = mixed.astype(jnp.float32)
    normed_two = rms_round(mixed_float)
    shard_part = lax.all_gather(w_gate_up, ("page", "tok"), axis=2, tiled=True)
    gate_vals = jnp.dot(normed_two, shard_part[0], preferred_element_type=jnp.float32)
    up_vals = jnp.dot(normed_two, shard_part[1], preferred_element_type=jnp.float32)
    hidden = (jax.nn.silu(gate_vals) * up_vals).astype(jnp.bfloat16)
    down_vals = jnp.dot(
        hidden,
        lax.all_gather(w_down, ("page", "tok"), axis=1, tiled=True),
        preferred_element_type=jnp.float32,
    )
    return (mixed_float + down_vals).astype(jnp.bfloat16)


def lane_relay(row_data, length, lane_index):
    row_count = row_data.shape[0]
    page_here = lax.axis_index("page")
    live_rows = jnp.clip(length - lane_index * row_count, 0, row_count)
    before = entering(live_rows.reshape(1), "page", add_counts, jnp.zeros((1,), jnp.int32))[0]
    distance = page_here * row_count - before
    in_shift = distance % row_count
    hop_count = distance // row_count
    row_ids = jnp.arange(row_count, dtype=jnp.int32)
    live_flag = row_ids < live_rows
    kept_data = jnp.where(live_flag[:, None], row_data, jnp.zeros_like(row_data))
    kept_tags = jnp.where(live_flag, hop_count + 1, 0).astype(jnp.int32)
    zero_data = jnp.zeros_like(row_data)
    zero_tags = jnp.zeros_like(kept_tags)
    here_data = lax.dynamic_slice_in_dim(
        jnp.concatenate([kept_data, zero_data], 0), in_shift, row_count, 0
    )
    here_tags = lax.dynamic_slice_in_dim(
        jnp.concatenate([kept_tags, zero_tags], 0), in_shift, row_count, 0
    )
    spill_data = lax.dynamic_slice_in_dim(
        jnp.concatenate([zero_data, kept_data], 0), in_shift, row_count, 0
    )
    spill_tags = lax.dynamic_slice_in_dim(
        jnp.concatenate([zero_tags, kept_tags], 0), in_shift, row_count, 0
    )
    got_data, got_tags = from_behind((spill_data, spill_tags), "page", -1)
    arrived = got_tags > 0
    cur_data = jnp.where(arrived[:, None], got_data, here_data)
    cur_tags = jnp.where(arrived, got_tags, here_tags)
    for bit_pos in range((lax.axis_size("page") - 1).bit_length()):
        stride_len = 1 << bit_pos
        present = cur_tags > 0
        moving = present & ((cur_tags - 1) // stride_len % 2 == 1)
        staying = present & jnp.logical_not(moving)
        out_data = jnp.where(moving[:, None], cur_data, jnp.zeros_like(cur_data))
        out_tags = jnp.where(moving, cur_tags, 0)
        got_data, got_tags = from_behind((out_data, out_tags), "page", -stride_len)
        arrived = got_tags > 0
        kept_now = jnp.where(staying[:, None], cur_data, jnp.zeros_like(cur_data))
        cur_data = jnp.where(arrived[:, None], got_data, kept_now)
        cur_tags = jnp.where(arrived, got_tags, jnp.where(staying, cur_tags, 0))
    return cur_data


def per_device(tile_tokens, page_lengths, occupancy, block_mix, stride_mix, w_gate_up, w_down):
    lane_index = lax.axis_index("tok")
    row_count = tile_tokens.shape[1]
    feat_width = tile_tokens.shape[2]
    blocks_here = block_mix.shape[0]
    blk_size = block_mix.shape[1]
    length = page_lengths[0]
    positions = lane_index * row_count + jnp.arange(row_count, dtype=jnp.int32)
    live_mask = (positions < length) & (jnp.repeat(occupancy[0], blk_size) > 0)
    masked = jnp.where(live_mask[:, None], tile_tokens[0].astype(jnp.float32), 0.0)
    normed = rms_round(masked).reshape(blocks_here, blk_size, feat_width)
    first = jnp.einsum(
        "bji,bic->bjc", block_mix, normed, preferred_element_type=jnp.float32
    ).astype(jnp.bfloat16)
    second = jnp.einsum(
        "jkb,bjc->jkc",
        stride_mix,
        lax.all_to_all(first, "tok", split_axis=1, concat_axis=0, tiled=True),
        preferred_element_type=jnp.float32,
    )
    mixed = (masked + second.reshape(row_count, feat_width)).astype(jnp.bfloat16)
    layer_out = channel_mlp(mixed, w_gate_up, w_down)
    packed = lane_relay(layer_out, length, lane_index)
    return packed.reshape(1, row_count, feat_width)


SMEM = pl.BlockSpec(memory_space=pltpu.SMEM)
VMEM = pl.BlockSpec(memory_space=pltpu.VMEM)
ANY = pl.BlockSpec(memory_space=pl.ANY)
MIB = 1024 * 1024
GROUP = 16
SUB = 8
SPANS = (2, 2, 2, 2)
TOKEN = jax.ShapeDtypeStruct((8, 128), jnp.int32)


def local_call(kernel, name, limit, in_specs, out_specs, out_shape, after=(), grid=(), scratch=()):
    ins, waits, outs = len(in_specs), len(after), len(out_specs)

    def body(*refs):
        token_ref = refs[ins + waits + outs]
        kernel(*refs[:ins], *refs[ins + waits:ins + waits + outs], *refs[ins + waits + outs + 1:])
        token_ref[...] = jnp.zeros(token_ref.shape, token_ref.dtype)

    token_spec = pl.BlockSpec(TOKEN.shape, lambda *_: (0, 0)) if grid else VMEM
    call = pl.pallas_call(
        body,
        grid=grid,
        in_specs=list(in_specs) + [ANY] * waits,
        out_specs=list(out_specs) + [token_spec],
        out_shape=list(out_shape) + [TOKEN],
        scratch_shapes=list(scratch),
        compiler_params=pltpu.CompilerParams(vmem_limit_bytes=limit * MIB),
        cost_estimate=pl.CostEstimate(flops=1, bytes_accessed=1, transcendentals=0),
        name=name,
    )

    def run(*operands):
        *results, token = call(*operands, *after)
        return results, token

    return run


def live_rows(start, shape, length, occupied):
    ids = start + lax.broadcasted_iota(jnp.int32, shape, 0)
    return (ids < length) & (occupied > 0)


def first_kernel(ids_ref, lengths_ref, occ_ref, tile_ref, mix_ref, *out_refs):
    step = pl.program_id(0)
    blocks, blk_size = mix_ref.shape[:2]
    feat_width = tile_ref.shape[2]
    lane = ids_ref[1]
    share = out_refs[0].shape[1]
    parts = blk_size // share
    rows_here = pl.num_programs(0) * blocks * blk_size
    for i in range(blocks):
        block = step * blocks + i
        start = lane * rows_here + block * blk_size
        live = live_rows(start, (blk_size, feat_width), lengths_ref[ids_ref[0]], occ_ref[0, block])
        tile = tile_ref[0, i * blk_size:(i + 1) * blk_size, :]
        masked = jnp.where(live, tile.astype(jnp.float32), 0.0)
        normed = rms_round(masked)
        picked = [mix_ref[i, pl.ds(pl.multiple_of((lane ^ part) * share, share), share), :] for part in range(parts)]
        mix = jnp.concatenate(picked, axis=0)
        first = jnp.dot(mix, normed, preferred_element_type=jnp.float32).astype(jnp.bfloat16)
        begin = 0
        for group in range(len(out_refs) // parts):
            end = begin + out_refs[group * parts].shape[2]
            for part in range(parts):
                out_refs[group * parts + part][i] = first[part * share:(part + 1) * share, begin:end]
            begin = end


def first_factor(ids, lengths, occupancy, tile_tokens, block_mix, parts, groups, after):
    blocks, blk_size, _ = block_mix.shape
    feat_width = tile_tokens.shape[2]
    share = blk_size // parts
    each = 2
    return local_call(
        first_kernel,
        "first_factor",
        16,
        [
            SMEM,
            SMEM,
            SMEM,
            pl.BlockSpec((1, each * blk_size, feat_width), lambda b: (0, b, 0)),
            pl.BlockSpec((each, blk_size, blk_size), lambda b: (b, 0, 0)),
        ],
        [pl.BlockSpec((each, share, width), lambda b: (b, 0, 0)) for width in groups for _ in range(parts)],
        [jax.ShapeDtypeStruct((blocks, share, width), jnp.bfloat16) for width in groups for _ in range(parts)],
        after,
        grid=(blocks // each,),
    )(ids, lengths, occupancy, tile_tokens, block_mix)


def spread_kernel(parts, ids_ref, stride_ref, out_ref):
    spots, outs, ins = stride_ref.shape
    rows, cols = GROUP * outs, GROUP * ins
    column = lax.broadcasted_iota(jnp.int32, (ins, cols), 1) // GROUP
    here = ins // parts
    block = ((column // here) ^ ids_ref[1]) * here + column % here
    picks = block == lax.broadcasted_iota(jnp.int32, (ins, cols), 0)
    picks = picks.astype(jnp.float32).astype(jnp.bfloat16)
    spot_row = lax.broadcasted_iota(jnp.int32, (rows, cols), 0) // outs
    spot_col = lax.broadcasted_iota(jnp.int32, (rows, cols), 1) % GROUP
    for group in range(spots // GROUP):
        flat = stride_ref[group * GROUP:(group + 1) * GROUP].reshape(rows, ins)
        wide = jnp.dot(flat, picks, preferred_element_type=jnp.float32)
        out_ref[group] = jnp.where(spot_row == spot_col, wide, 0.0).astype(jnp.bfloat16)


def spread_stride(ids, stride_mix, parts, after):
    spots, outs, ins = stride_mix.shape
    shape = jax.ShapeDtypeStruct((spots // GROUP, GROUP * outs, GROUP * ins), jnp.bfloat16)
    kernel = functools.partial(spread_kernel, parts)
    return local_call(kernel, "spread_stride", 12, [SMEM, VMEM], [VMEM], [shape], after)(ids, stride_mix)


def kept_of(length, lane, rows):
    return jnp.clip(length - lane * rows, 0, rows)


def offset_of(lengths_ref, page, lane, rows):
    total = jnp.int32(0)
    for earlier in range(lengths_ref.shape[0]):
        total += jnp.where(earlier < page, kept_of(lengths_ref[earlier], lane, rows), 0)
    return total


def second_kernel(parts, begin, ids_ref, lengths_ref, occ_ref, spread_ref, *refs):
    first_refs, tile_ref, out_refs, twice_ref = refs[:parts], refs[parts], refs[parts + 1:-1], refs[-1]
    rows, width = tile_ref.shape[1], first_refs[0].shape[2]
    page, lane = ids_ref[0], ids_ref[1]
    length = lengths_ref[page]
    groups, group_rows, depth = spread_ref.shape
    blk_size = rows // occ_ref.shape[1]
    for group in range(groups):
        values = [ref[:, group * GROUP:(group + 1) * GROUP, :].reshape(depth // parts, width) for ref in first_refs]
        second = jnp.dot(spread_ref[group], jnp.concatenate(values, axis=0), preferred_element_type=jnp.float32)
        for part in range(group_rows // blk_size):
            at = group * group_rows + part * blk_size
            live = live_rows(lane * rows + at, (blk_size, width), length, occ_ref[0, at // blk_size])
            tile = tile_ref[0, at:at + blk_size, begin:begin + width]
            masked = jnp.where(live, tile.astype(jnp.float32), 0.0)
            mixed = masked + second[part * blk_size:(part + 1) * blk_size]
            mixed = mixed.astype(jnp.bfloat16).astype(jnp.float32)
            twice_ref[at:at + blk_size, :] = mixed
            twice_ref[rows + at:rows + at + blk_size, :] = mixed
    twice_ref[2 * rows:, :] = jnp.zeros((SUB, width), jnp.float32)
    start = rows - offset_of(lengths_ref, page, lane, rows) % rows
    extra = start % SUB
    base = pl.multiple_of(start - extra, SUB)
    tall = twice_ref[pl.ds(base, rows + SUB), :].reshape(rows // SUB + 1, SUB, width)
    tall = pltpu.roll(tall, (SUB - extra) % SUB, 1)
    inside = lax.broadcasted_iota(jnp.int32, (1, SUB, width), 1) + extra < SUB
    turned = jnp.where(inside, tall[:-1], tall[1:]).reshape(rows, width).astype(jnp.bfloat16)
    begin = 0
    for out_ref in out_refs:
        end = begin + out_ref.shape[1]
        out_ref[...] = turned[:, begin:end]
        begin = end


def second_factor(begin, spans, ids, lengths, occupancy, spread, firsts, tile_tokens, after):
    rows = tile_tokens.shape[1]
    width = firsts[0].shape[2]
    parts = len(firsts)
    return local_call(
        functools.partial(second_kernel, parts, begin),
        "second_factor",
        24,
        [SMEM, SMEM, SMEM, VMEM] + [VMEM] * parts + [VMEM],
        [VMEM] * len(spans),
        [jax.ShapeDtypeStruct((rows, span), jnp.bfloat16) for span in spans],
        after,
        scratch=[pltpu.VMEM((2 * rows + SUB, width), jnp.float32)],
    )(ids, lengths, occupancy, spread, *firsts, tile_tokens)


def pick(mask, yes_ref, no_ref):
    return jnp.where(mask, yes_ref[...].astype(jnp.float32), no_ref[...].astype(jnp.float32))


def parity_kernel(ids_ref, lengths_ref, own_ref, got_ref, out_ref):
    rows = own_ref.shape[0]
    page, lane = ids_ref[0], ids_ref[1]
    offset = offset_of(lengths_ref, page, lane, rows)
    kept = kept_of(lengths_ref[page], lane, rows)
    slot = lax.broadcasted_iota(jnp.int32, own_ref.shape, 0)
    base, shift = offset // rows, offset % rows
    early = (base % 2 == page % 2).astype(jnp.int32)
    low = jnp.where(early == 1, shift, 0)
    high = jnp.where(early == 1, jnp.minimum(shift + kept, rows), shift + kept - rows)
    out_ref[...] = pick((slot >= low) & (slot < high), own_ref, got_ref).astype(out_ref.dtype)


def join_parity(ids, lengths, own, got, after):
    shape = jax.ShapeDtypeStruct(own.shape, own.dtype)
    return local_call(parity_kernel, "join_parity", 6, [SMEM, SMEM, VMEM, VMEM], [VMEM], [shape], after)(ids, lengths, own, got)


def forward_kernel(ids_ref, lengths_ref, own_ref, one_ref, two_ref, out_ref):
    rows = own_ref.shape[0]
    page, lane = ids_ref[0], ids_ref[1]
    level = page // 2
    slot = (page % 2) * rows + lax.broadcasted_iota(jnp.int32, own_ref.shape, 0)
    after_one = offset_of(lengths_ref, 2 * level + 2, lane, rows)
    after_two = offset_of(lengths_ref, 2 * level + 4, lane, rows)
    value = pick(slot < after_two, one_ref, two_ref)
    out_ref[...] = jnp.where(slot < after_one, own_ref[...].astype(jnp.float32), value).astype(out_ref.dtype)


def forward_merge(ids, lengths, own, one, two, after):
    shape = jax.ShapeDtypeStruct(own.shape, own.dtype)
    specs = [SMEM, SMEM, VMEM, VMEM, VMEM]
    return local_call(forward_kernel, "forward_merge", 6, specs, [VMEM], [shape], after)(ids, lengths, own, one, two)


def final_kernel(ids_ref, lengths_ref, own_ref, one_ref, two_ref, last_ref, out_ref):
    rows = own_ref.shape[0]
    page, lane = ids_ref[0], ids_ref[1]
    level = page // 2
    slot = page * rows + lax.broadcasted_iota(jnp.int32, own_ref.shape, 0)
    ends = [offset_of(lengths_ref, 2 * (level + ahead), lane, rows) for ahead in (1, 2)]
    total = offset_of(lengths_ref, lengths_ref.shape[0], lane, rows)

    @pl.when(level == 0)
    def _():
        value = pick(slot < ends[0], own_ref, last_ref)
        out_ref[...] = jnp.where(slot < total, value, 0.0).astype(out_ref.dtype)

    @pl.when(level > 0)
    def _():
        value = pick(slot < ends[1], one_ref, two_ref)
        value = jnp.where(slot < ends[0], own_ref[...].astype(jnp.float32), value)
        out_ref[...] = jnp.where(slot < total, value, 0.0).astype(out_ref.dtype)


def final_merge(ids, lengths, own, one, two, last, after):
    shape = jax.ShapeDtypeStruct(own.shape, own.dtype)
    specs = [SMEM, SMEM, VMEM, VMEM, VMEM, VMEM]
    return local_call(final_kernel, "final_merge", 8, specs, [VMEM], [shape], after)(ids, lengths, own, one, two, last)


def mlp_kernel(pieces, *refs):
    sources, refs = refs[:pieces], refs[pieces:]
    main_ref, out_ref, gate_ref, up_ref, down_ref, sems = refs
    step = pl.program_id(0)
    here, levels = main_ref.shape[:2]
    hidden_width, feat_width = gate_ref.shape
    wide, thin = hidden_width // (here * levels), feat_width // (here * levels)
    parts = levels
    span = hidden_width // parts
    gates = gate_ref.reshape(levels, here, wide, feat_width)
    ups = up_ref.reshape(levels, here, wide, feat_width)
    downs = down_ref.reshape(levels, here, thin, hidden_width)

    def copies(part):
        begin = part * span
        at, cols = 2 * wide + begin // feat_width * thin, pl.ds(begin % feat_width, span)
        found = [(main_ref.at[:, part, :wide], gates.at[part]), (main_ref.at[:, part, wide:2 * wide], ups.at[part])]
        for level in range(levels):
            found.append((main_ref.at[:, level, at:at + thin, cols], downs.at[level, :, :, begin:begin + span]))
        return [pltpu.make_async_copy(src, dst, sems.at[part, i]) for i, (src, dst) in enumerate(found)]

    @pl.when(step == 0)
    def _():
        for part in range(parts):
            for copy in copies(part):
                copy.start()

    mixed = jnp.concatenate([ref[...] for ref in sources], axis=1).astype(jnp.float32)
    normed = rms_round(mixed)
    contract = (((1,), (1,)), ((), ()))
    result = mixed
    for part in range(parts):
        @pl.when(step == 0)
        def _():
            for copy in copies(part):
                copy.wait()

        at = part * span
        gate = lax.dot_general(normed, gate_ref[at:at + span, :], contract, preferred_element_type=jnp.float32)
        up = lax.dot_general(normed, up_ref[at:at + span, :], contract, preferred_element_type=jnp.float32)
        hidden = (gate / (1.0 + jnp.exp(-gate)) * up).astype(jnp.bfloat16)
        down = down_ref[:, at:at + span]
        result += lax.dot_general(hidden, down, contract, preferred_element_type=jnp.float32)
    out_ref[0] = result.astype(out_ref.dtype)


def packed_mlp(sources, weights):
    rows = sources[0].shape[0]
    pieces = len(sources)
    here, levels, each, feat_width = weights.shape
    hidden_width = here * levels * (each - feat_width // (here * levels) * 2) // 2
    steps = 2
    block = rows // steps
    return pl.pallas_call(
        functools.partial(mlp_kernel, pieces),
        grid=(steps,),
        in_specs=[pl.BlockSpec((block, source.shape[1]), lambda i: (i, 0)) for source in sources] + [ANY],
        out_specs=pl.BlockSpec((1, block, feat_width), lambda i: (0, i, 0)),
        out_shape=jax.ShapeDtypeStruct((1, rows, feat_width), jnp.bfloat16),
        scratch_shapes=[
            pltpu.VMEM((hidden_width, feat_width), jnp.bfloat16),
            pltpu.VMEM((hidden_width, feat_width), jnp.bfloat16),
            pltpu.VMEM((feat_width, hidden_width), jnp.bfloat16),
            pltpu.SemaphoreType.DMA((levels, 2 + levels)),
        ],
        compiler_params=pltpu.CompilerParams(vmem_limit_bytes=40 * MIB),
        name="packed_mlp",
    )(*sources, weights)


def swap(value, axis, bit):
    return lax.ppermute(value, axis, [(i, i ^ bit) for i in range(lax.axis_size(axis))])


def pack_kernel(main_ref, down_ref, out_ref):
    wide, feat_width = main_ref.shape[1:]
    thin = down_ref.shape[0]
    out_ref[:wide] = main_ref[0]
    out_ref[wide:2 * wide] = main_ref[1]
    for part in range(down_ref.shape[1] // feat_width):
        at = 2 * wide + part * thin
        out_ref[at:at + thin] = down_ref[:, part * feat_width:(part + 1) * feat_width]


def pack_weights(main, down, after):
    _, wide, feat_width = main.shape
    rows = 2 * wide + down.size // feat_width
    shape = jax.ShapeDtypeStruct((rows, feat_width), main.dtype)
    return local_call(pack_kernel, "pack_weights", 6, [VMEM, VMEM], [VMEM], [shape], after)(main, down)


def pair_kernel(which, place, ids_ref, own_ref, got_ref, out_ref, both_ref, sems):
    axis, shift = which
    bit = (ids_ref[axis] // shift) % 2
    lead = (slice(None),) * place
    copies = [
        pltpu.make_async_copy(own_ref, both_ref.at[lead + (bit,)], sems.at[0]),
        pltpu.make_async_copy(got_ref, both_ref.at[lead + (1 - bit,)], sems.at[1]),
    ]
    for copy in copies:
        copy.start()
    for copy in copies:
        copy.wait()
    whole = pltpu.make_async_copy(both_ref, out_ref, sems.at[2])
    whole.start()
    whole.wait()


def pair_up(ids, own, got, which, place, after):
    shape = own.shape[:place] + (2,) + own.shape[place:]
    return local_call(
        functools.partial(pair_kernel, which, place),
        "pair_up",
        8,
        [SMEM, ANY, ANY],
        [ANY],
        [jax.ShapeDtypeStruct(shape, own.dtype)],
        after,
        scratch=[pltpu.VMEM(shape, own.dtype), pltpu.SemaphoreType.DMA((3,))],
    )(ids, own, got)


AXES = ("page", "tok")


def some_lengths(length, bit, least):
    pages = lax.axis_size("page")
    lengths = jnp.where(jnp.arange(pages) == lax.axis_index("page"), length, 0)
    while bit > least:
        lengths = lengths + swap(lengths, "page", bit)
        bit //= 2
    return lengths


def packed_device(tile_tokens, page_lengths, occupancy, block_mix, stride_mix, w_gate_up, w_down):
    ids = jnp.stack([lax.axis_index("page"), lax.axis_index("tok")]).astype(jnp.int32)
    pages, parts = lax.axis_size("page"), lax.axis_size("tok")
    feat_width = tile_tokens.shape[2]
    spans = [feat_width * eighths // 8 for eighths in SPANS]
    groups = (spans[0], feat_width - spans[0])
    z_far, z_near = (0, 4), (0, 2)
    tokens = []

    def chained(step, *operands):
        results, token = step(*operands, tokens[-1:])
        tokens.append(token)
        return results

    def paired(value, which, place):
        axis, shift = which
        return chained(pair_up, ids, value, swap(value, AXES[axis], shift), which, place)[0]

    def plane(value):
        here = 2 * parts
        groups = [[level * here + i for i in range(here)] for level in range(pages // 2)]
        return lax.all_gather(value.reshape((-1,) + value.shape[2:]), AXES, axis_index_groups=groups)

    def across(firsts):
        return firsts[:1] + [swap(firsts[part], "tok", part) for part in range(1, parts)]

    far_lengths = some_lengths(page_lengths[0], pages // 2, 1)
    tokens.append(far_lengths)
    weights = chained(pack_weights, jnp.swapaxes(w_gate_up, 1, 2), jnp.swapaxes(w_down, 0, 1))[0]
    lengths = far_lengths + swap(far_lengths, "page", 1)
    firsts = chained(first_factor, ids, lengths, occupancy, tile_tokens, block_mix, parts, groups)
    found = [across(firsts[:parts]), across(firsts[parts:])]
    spread = chained(spread_stride, ids, stride_mix, parts)[0]
    turned = chained(second_factor, 0, spans[:1], ids, lengths, occupancy, spread, found[0], tile_tokens)
    weights = paired(weights, z_far, 0)
    swapped = [swap(own, "page", 1) for own in turned]
    current, one, two, last, sources = {}, {}, {}, {}, []

    def join(k):
        current[k] = chained(join_parity, ids, lengths, turned[k], swapped[k])[0]
        one[k] = lax.ppermute(current[k], "page", [(4, 2), (5, 3), (6, 4), (7, 5), (2, 6), (3, 7)])
        two[k] = lax.ppermute(current[k], "page", [(6, 2), (7, 3), (2, 6), (3, 7)])

    def forward(k):
        merged = chained(forward_merge, ids, lengths, current[k], one[k], two[k])[0]
        last[k] = lax.ppermute(merged, "page", [(2, 0), (3, 1), (0, 2), (1, 3)])

    def finish(k):
        sources.extend(chained(final_merge, ids, lengths, current[k], one[k], two[k], last[k]))

    join(0)
    turned += chained(second_factor, spans[0], spans[1:], ids, lengths, occupancy, spread, found[1], tile_tokens)
    swapped += [swap(own, "page", 1) for own in turned[1:]]
    weights = plane(paired(weights, z_near, 1))
    join(1)
    count = len(spans)
    for k in range(count):
        forward(k)
        if k + 2 < count:
            join(k + 2)
        if k:
            finish(k - 1)
    finish(count - 1)
    return packed_mlp(sources, weights)


def solution(mesh):
    pages, parts = mesh.shape["page"], mesh.shape["tok"]
    return jax.shard_map(
        packed_device if (pages, parts) == (8, 4) else per_device,
        mesh=mesh,
        in_specs=(
            P("page", "tok", None),
            P("page"),
            P("page", "tok"),
            P("tok", None, None),
            P("tok", None, None),
            P(None, None, ("page", "tok")),
            P(None, ("page", "tok")),
        ),
        out_specs=P("tok", "page", None),
        check_vma=False,
    )
```

```python
import functools

import jax
import jax.numpy as jnp
from jax import lax
from jax.experimental import pallas as pl
from jax.experimental.pallas import tpu as pltpu
from jax.sharding import PartitionSpec as P

epsilon = 1e-05


def entering(value, axis, join, neutral):
    count, mine = (lax.axis_size(axis), lax.axis_index(axis))
    pieces = lax.all_gather(value, axis)
    so_far = jnp.full_like(value, 0) + jnp.asarray(neutral, value.dtype)

    def hop(position, so_far):
        longer = join(so_far, pieces[position])
        return jnp.where(position < mine, longer, so_far)

    return lax.fori_loop(0, count - 1, hop, so_far)


def from_behind(value, axis, by):
    length = lax.axis_size(axis)
    pairs = [(i, i + by) for i in range(length) if 0 <= i + by < length]
    return lax.ppermute(value, axis, pairs)


def rms_round(values):
    scale = lax.rsqrt(jnp.mean(values * values, axis=-1, keepdims=True) + epsilon)
    return (values * scale).astype(jnp.bfloat16)


def add_counts(earlier, later):
    return earlier + later


def channel_mlp(mixed, w_gate_up, w_down):
    mixed_float = mixed.astype(jnp.float32)
    normed_two = rms_round(mixed_float)
    shard_part = lax.all_gather(w_gate_up, ("page", "tok"), axis=2, tiled=True)
    gate_vals = jnp.dot(normed_two, shard_part[0], preferred_element_type=jnp.float32)
    up_vals = jnp.dot(normed_two, shard_part[1], preferred_element_type=jnp.float32)
    hidden = (jax.nn.silu(gate_vals) * up_vals).astype(jnp.bfloat16)
    down_vals = jnp.dot(
        hidden,
        lax.all_gather(w_down, ("page", "tok"), axis=1, tiled=True),
        preferred_element_type=jnp.float32,
    )
    return (mixed_float + down_vals).astype(jnp.bfloat16)


def lane_relay(row_data, length, lane_index):
    row_count = row_data.shape[0]
    page_here = lax.axis_index("page")
    live_rows = jnp.clip(length - lane_index * row_count, 0, row_count)
    before = entering(live_rows.reshape(1), "page", add_counts, jnp.zeros((1,), jnp.int32))[0]
    distance = page_here * row_count - before
    in_shift = distance % row_count
    hop_count = distance // row_count
    row_ids = jnp.arange(row_count, dtype=jnp.int32)
    live_flag = row_ids < live_rows
    kept_data = jnp.where(live_flag[:, None], row_data, jnp.zeros_like(row_data))
    kept_tags = jnp.where(live_flag, hop_count + 1, 0).astype(jnp.int32)
    zero_data = jnp.zeros_like(row_data)
    zero_tags = jnp.zeros_like(kept_tags)
    here_data = lax.dynamic_slice_in_dim(
        jnp.concatenate([kept_data, zero_data], 0), in_shift, row_count, 0
    )
    here_tags = lax.dynamic_slice_in_dim(
        jnp.concatenate([kept_tags, zero_tags], 0), in_shift, row_count, 0
    )
    spill_data = lax.dynamic_slice_in_dim(
        jnp.concatenate([zero_data, kept_data], 0), in_shift, row_count, 0
    )
    spill_tags = lax.dynamic_slice_in_dim(
        jnp.concatenate([zero_tags, kept_tags], 0), in_shift, row_count, 0
    )
    got_data, got_tags = from_behind((spill_data, spill_tags), "page", -1)
    arrived = got_tags > 0
    cur_data = jnp.where(arrived[:, None], got_data, here_data)
    cur_tags = jnp.where(arrived, got_tags, here_tags)
    for bit_pos in range((lax.axis_size("page") - 1).bit_length()):
        stride_len = 1 << bit_pos
        present = cur_tags > 0
        moving = present & ((cur_tags - 1) // stride_len % 2 == 1)
        staying = present & jnp.logical_not(moving)
        out_data = jnp.where(moving[:, None], cur_data, jnp.zeros_like(cur_data))
        out_tags = jnp.where(moving, cur_tags, 0)
        got_data, got_tags = from_behind((out_data, out_tags), "page", -stride_len)
        arrived = got_tags > 0
        kept_now = jnp.where(staying[:, None], cur_data, jnp.zeros_like(cur_data))
        cur_data = jnp.where(arrived[:, None], got_data, kept_now)
        cur_tags = jnp.where(arrived, got_tags, jnp.where(staying, cur_tags, 0))
    return cur_data


def per_device(tile_tokens, page_lengths, occupancy, block_mix, stride_mix, w_gate_up, w_down):
    lane_index = lax.axis_index("tok")
    row_count = tile_tokens.shape[1]
    feat_width = tile_tokens.shape[2]
    blocks_here = block_mix.shape[0]
    blk_size = block_mix.shape[1]
    length = page_lengths[0]
    positions = lane_index * row_count + jnp.arange(row_count, dtype=jnp.int32)
    live_mask = (positions < length) & (jnp.repeat(occupancy[0], blk_size) > 0)
    masked = jnp.where(live_mask[:, None], tile_tokens[0].astype(jnp.float32), 0.0)
    normed = rms_round(masked).reshape(blocks_here, blk_size, feat_width)
    first = jnp.einsum(
        "bji,bic->bjc", block_mix, normed, preferred_element_type=jnp.float32
    ).astype(jnp.bfloat16)
    second = jnp.einsum(
        "jkb,bjc->jkc",
        stride_mix,
        lax.all_to_all(first, "tok", split_axis=1, concat_axis=0, tiled=True),
        preferred_element_type=jnp.float32,
    )
    mixed = (masked + second.reshape(row_count, feat_width)).astype(jnp.bfloat16)
    layer_out = channel_mlp(mixed, w_gate_up, w_down)
    packed = lane_relay(layer_out, length, lane_index)
    return packed.reshape(1, row_count, feat_width)


SMEM = pl.BlockSpec(memory_space=pltpu.SMEM)
VMEM = pl.BlockSpec(memory_space=pltpu.VMEM)
ANY = pl.BlockSpec(memory_space=pl.ANY)
MIB = 1024 * 1024
GROUP = 16
BLOCKS = 2
MLP_MIB = 30
SUB = 8
SPANS = (2, 2, 2, 2)
BRIEF = 1
TOKEN = jax.ShapeDtypeStruct((8, 128), jnp.int32)


def local_call(kernel, name, limit, in_specs, out_specs, out_shape, after, grid=(), scratch=()):
    after, cost = after
    ins, waits, outs = len(in_specs), len(after), len(out_specs)

    def body(*refs):
        token_ref = refs[ins + waits + outs]
        kernel(*refs[:ins], *refs[ins + waits:ins + waits + outs], *refs[ins + waits + outs + 1:])
        token_ref[...] = jnp.zeros(token_ref.shape, token_ref.dtype)

    token_spec = pl.BlockSpec(TOKEN.shape, lambda *_: (0, 0)) if grid else VMEM
    call = pl.pallas_call(
        body,
        grid=grid,
        in_specs=list(in_specs) + [ANY] * waits,
        out_specs=list(out_specs) + [token_spec],
        out_shape=list(out_shape) + [TOKEN],
        scratch_shapes=list(scratch),
        compiler_params=pltpu.CompilerParams(vmem_limit_bytes=limit * MIB),
        cost_estimate=pl.CostEstimate(flops=cost, bytes_accessed=cost // 1000, transcendentals=0),
        name=name,
    )

    def run(*operands):
        *results, token = call(*operands, *after)
        return results, token

    return run


def live_rows(start, shape, length, occupied):
    ids = start + lax.broadcasted_iota(jnp.int32, shape, 0)
    return (ids < length) & (occupied > 0)


def first_kernel(ids_ref, length_ref, occ_ref, tile_ref, mix_ref, *out_refs):
    step = pl.program_id(0)
    blocks, blk_size = mix_ref.shape[:2]
    feat_width = tile_ref.shape[2]
    lane = ids_ref[1]
    share = out_refs[0].shape[1]
    parts = blk_size // share
    rows_here = pl.num_programs(0) * blocks * blk_size
    for i in range(blocks):
        block = step * blocks + i
        start = lane * rows_here + block * blk_size
        live = live_rows(start, (blk_size, feat_width), length_ref[0], occ_ref[0, block])
        tile = tile_ref[0, i * blk_size:(i + 1) * blk_size, :]
        masked = jnp.where(live, tile.astype(jnp.float32), 0.0)
        normed = rms_round(masked)
        picked = [mix_ref[i, pl.ds(pl.multiple_of((lane ^ part) * share, share), share), :] for part in range(parts)]
        mix = jnp.concatenate(picked, axis=0)
        first = jnp.dot(mix, normed, preferred_element_type=jnp.float32).astype(jnp.bfloat16)
        begin = 0
        for group in range(len(out_refs) // parts):
            end = begin + out_refs[group * parts].shape[2]
            for part in range(parts):
                out_refs[group * parts + part][i] = first[part * share:(part + 1) * share, begin:end]
            begin = end


def first_factor(ids, length, occupancy, tile_tokens, block_mix, parts, groups, after):
    blocks, blk_size, _ = block_mix.shape
    feat_width = tile_tokens.shape[2]
    share = blk_size // parts
    each = 2
    return local_call(
        first_kernel,
        "first_factor",
        16,
        [
            SMEM,
            SMEM,
            SMEM,
            pl.BlockSpec((1, each * blk_size, feat_width), lambda b: (0, b, 0)),
            pl.BlockSpec((each, blk_size, blk_size), lambda b: (b, 0, 0)),
        ],
        [pl.BlockSpec((each, share, width), lambda b: (b, 0, 0)) for width in groups for _ in range(parts)],
        [jax.ShapeDtypeStruct((blocks, share, width), jnp.bfloat16) for width in groups for _ in range(parts)],
        after,
        grid=(blocks // each,),
    )(ids, length, occupancy, tile_tokens, block_mix)


def spread_kernel(parts, ids_ref, stride_ref, out_ref):
    spots, outs, ins = stride_ref.shape
    rows, cols = GROUP * outs, GROUP * ins
    column = lax.broadcasted_iota(jnp.int32, (ins, cols), 1) // GROUP
    here = ins // parts
    block = ((column // here) ^ ids_ref[1]) * here + column % here
    picks = block == lax.broadcasted_iota(jnp.int32, (ins, cols), 0)
    picks = picks.astype(jnp.float32).astype(jnp.bfloat16)
    spot_row = lax.broadcasted_iota(jnp.int32, (rows, cols), 0) // outs
    spot_col = lax.broadcasted_iota(jnp.int32, (rows, cols), 1) % GROUP
    for group in range(spots // GROUP):
        flat = stride_ref[group * GROUP:(group + 1) * GROUP].reshape(rows, ins)
        wide = jnp.dot(flat, picks, preferred_element_type=jnp.float32)
        out_ref[group] = jnp.where(spot_row == spot_col, wide, 0.0).astype(jnp.bfloat16)


def spread_stride(ids, stride_mix, parts, after):
    spots, outs, ins = stride_mix.shape
    shape = jax.ShapeDtypeStruct((spots // GROUP, GROUP * outs, GROUP * ins), jnp.bfloat16)
    kernel = functools.partial(spread_kernel, parts)
    return local_call(kernel, "spread_stride", 12, [SMEM, VMEM], [VMEM], [shape], after)(ids, stride_mix)


def kept_of(length, lane, rows):
    return jnp.clip(length - lane * rows, 0, rows)


def offset_of(lengths_ref, page, lane, rows):
    total = jnp.int32(0)
    for earlier in range(lengths_ref.shape[0]):
        total += jnp.where(earlier < page, kept_of(lengths_ref[earlier], lane, rows), 0)
    return total


def second_kernel(parts, begin, ids_ref, lengths_ref, occ_ref, spread_ref, *refs):
    first_refs, tile_ref, out_refs, twice_ref = refs[:parts], refs[parts], refs[parts + 1:-1], refs[-1]
    rows, width = tile_ref.shape[1], first_refs[0].shape[2]
    page, lane = ids_ref[0], ids_ref[1]
    length = lengths_ref[page]
    groups, group_rows, depth = spread_ref.shape
    blk_size = rows // occ_ref.shape[1]
    for group in range(groups):
        values = [ref[:, group * GROUP:(group + 1) * GROUP, :].reshape(depth // parts, width) for ref in first_refs]
        second = jnp.dot(spread_ref[group], jnp.concatenate(values, axis=0), preferred_element_type=jnp.float32)
        for part in range(group_rows // blk_size):
            at = group * group_rows + part * blk_size
            live = live_rows(lane * rows + at, (blk_size, width), length, occ_ref[0, at // blk_size])
            tile = tile_ref[0, at:at + blk_size, begin:begin + width]
            masked = jnp.where(live, tile.astype(jnp.float32), 0.0)
            mixed = masked + second[part * blk_size:(part + 1) * blk_size]
            mixed = mixed.astype(jnp.bfloat16).astype(jnp.float32)
            twice_ref[at:at + blk_size, :] = mixed
            twice_ref[rows + at:rows + at + blk_size, :] = mixed
    twice_ref[2 * rows:, :] = jnp.zeros((SUB, width), jnp.float32)
    start = rows - offset_of(lengths_ref, page, lane, rows) % rows
    extra = start % SUB
    base = pl.multiple_of(start - extra, SUB)
    tall = twice_ref[pl.ds(base, rows + SUB), :].reshape(rows // SUB + 1, SUB, width)
    tall = pltpu.roll(tall, (SUB - extra) % SUB, 1)
    inside = lax.broadcasted_iota(jnp.int32, (1, SUB, width), 1) + extra < SUB
    turned = jnp.where(inside, tall[:-1], tall[1:]).reshape(rows, width).astype(jnp.bfloat16)
    begin = 0
    for out_ref in out_refs:
        end = begin + out_ref.shape[1]
        out_ref[...] = turned[:, begin:end]
        begin = end


def second_factor(begin, spans, ids, lengths, occupancy, spread, firsts, tile_tokens, after):
    rows = tile_tokens.shape[1]
    width = firsts[0].shape[2]
    parts = len(firsts)
    return local_call(
        functools.partial(second_kernel, parts, begin),
        "second_factor",
        24,
        [SMEM, SMEM, SMEM, VMEM] + [VMEM] * parts + [VMEM],
        [VMEM] * len(spans),
        [jax.ShapeDtypeStruct((rows, span), jnp.bfloat16) for span in spans],
        after,
        scratch=[pltpu.VMEM((2 * rows + SUB, width), jnp.float32)],
    )(ids, lengths, occupancy, spread, *firsts, tile_tokens)


def pick(mask, yes_ref, no_ref):
    return jnp.where(mask, yes_ref[...].astype(jnp.float32), no_ref[...].astype(jnp.float32))


def parity_kernel(ids_ref, lengths_ref, own_ref, got_ref, out_ref):
    rows = own_ref.shape[0]
    page, lane = ids_ref[0], ids_ref[1]
    offset = offset_of(lengths_ref, page, lane, rows)
    kept = kept_of(lengths_ref[page], lane, rows)
    slot = lax.broadcasted_iota(jnp.int32, own_ref.shape, 0)
    base, shift = offset // rows, offset % rows
    early = (base % 2 == page % 2).astype(jnp.int32)
    low = jnp.where(early == 1, shift, 0)
    high = jnp.where(early == 1, jnp.minimum(shift + kept, rows), shift + kept - rows)
    out_ref[...] = pick((slot >= low) & (slot < high), own_ref, got_ref).astype(out_ref.dtype)


def join_parity(ids, lengths, own, got, after):
    shape = jax.ShapeDtypeStruct(own.shape, own.dtype)
    return local_call(parity_kernel, "join_parity", 6, [SMEM, SMEM, VMEM, VMEM], [VMEM], [shape], after)(ids, lengths, own, got)


def forward_kernel(ids_ref, lengths_ref, own_ref, one_ref, two_ref, out_ref):
    rows = own_ref.shape[0]
    page, lane = ids_ref[0], ids_ref[1]
    level = page // 2
    slot = (page % 2) * rows + lax.broadcasted_iota(jnp.int32, own_ref.shape, 0)
    after_one = offset_of(lengths_ref, 2 * level + 2, lane, rows)
    after_two = offset_of(lengths_ref, 2 * level + 4, lane, rows)
    value = pick(slot < after_two, one_ref, two_ref)
    out_ref[...] = jnp.where(slot < after_one, own_ref[...].astype(jnp.float32), value).astype(out_ref.dtype)


def forward_merge(ids, lengths, own, one, two, after):
    shape = jax.ShapeDtypeStruct(own.shape, own.dtype)
    specs = [SMEM, SMEM, VMEM, VMEM, VMEM]
    return local_call(forward_kernel, "forward_merge", 6, specs, [VMEM], [shape], after)(ids, lengths, own, one, two)


def final_kernel(ids_ref, lengths_ref, own_ref, one_ref, two_ref, last_ref, out_ref):
    rows = own_ref.shape[0]
    page, lane = ids_ref[0], ids_ref[1]
    level = page // 2
    slot = page * rows + lax.broadcasted_iota(jnp.int32, own_ref.shape, 0)
    ends = [offset_of(lengths_ref, 2 * (level + ahead), lane, rows) for ahead in (1, 2)]
    total = offset_of(lengths_ref, lengths_ref.shape[0], lane, rows)

    @pl.when(level == 0)
    def _():
        value = pick(slot < ends[0], own_ref, last_ref)
        out_ref[...] = jnp.where(slot < total, value, 0.0).astype(out_ref.dtype)

    @pl.when(level > 0)
    def _():
        value = pick(slot < ends[1], one_ref, two_ref)
        value = jnp.where(slot < ends[0], own_ref[...].astype(jnp.float32), value)
        out_ref[...] = jnp.where(slot < total, value, 0.0).astype(out_ref.dtype)


def final_merge(ids, lengths, own, one, two, last, after):
    shape = jax.ShapeDtypeStruct(own.shape, own.dtype)
    specs = [SMEM, SMEM, VMEM, VMEM, VMEM, VMEM]
    return local_call(final_kernel, "final_merge", 8, specs, [VMEM], [shape], after)(ids, lengths, own, one, two, last)


NT = (((1,), (1,)), ((), ()))


def mlp_kernel(pieces, *refs):
    sources, (main_ref, out_ref) = refs[:pieces], refs[pieces:]
    here, levels, each, feat_width = main_ref.shape
    thin = feat_width // (here * levels)
    wide = (each - 2 * thin) // 2
    rows = out_ref.shape[1]
    block = rows // BLOCKS

    def weights(level, begin, count):
        return main_ref[:, level, begin:begin + count, :].reshape(here * count, feat_width)

    def times(values, matrix):
        return lax.dot_general(values, matrix, NT, preferred_element_type=jnp.float32)

    for at in range(0, rows, block):
        mixed = jnp.concatenate([ref[at:at + block, :] for ref in sources], axis=1).astype(jnp.float32)
        normed = rms_round(mixed)
        hidden = []
        for level in range(levels):
            gate = times(normed, weights(level, 0, wide))
            up = times(normed, weights(level, wide, wide))
            hidden.append((gate / (1.0 + jnp.exp(-gate)) * up).astype(jnp.bfloat16))
        hidden = jnp.concatenate(hidden, axis=1)
        halves = hidden.shape[1] // feat_width
        for level in range(levels):
            cols = slice(level * here * thin, (level + 1) * here * thin)
            result = mixed[:, cols]
            for part in range(halves):
                inner = hidden[:, part * feat_width:(part + 1) * feat_width]
                result += times(inner, weights(level, 2 * wide + part * thin, thin))
            out_ref[0, at:at + block, cols] = result.astype(out_ref.dtype)


def packed_mlp(sources, weights):
    rows, feat_width = sources[0].shape[0], weights.shape[3]
    return pl.pallas_call(
        functools.partial(mlp_kernel, len(sources)),
        in_specs=[VMEM] * (len(sources) + 1),
        out_specs=VMEM,
        out_shape=jax.ShapeDtypeStruct((1, rows, feat_width), jnp.bfloat16),
        compiler_params=pltpu.CompilerParams(vmem_limit_bytes=MLP_MIB * MIB),
        name="packed_mlp",
    )(*sources, weights)


def swap(value, axis, bit):
    return lax.ppermute(value, axis, [(i, i ^ bit) for i in range(lax.axis_size(axis))])


def pack_kernel(main_ref, down_ref, out_ref):
    wide, feat_width = main_ref.shape[1:]
    thin = down_ref.shape[0]
    out_ref[:wide] = main_ref[0]
    out_ref[wide:2 * wide] = main_ref[1]
    for part in range(down_ref.shape[1] // feat_width):
        at = 2 * wide + part * thin
        out_ref[at:at + thin] = down_ref[:, part * feat_width:(part + 1) * feat_width]


def pack_weights(main, down, after):
    _, wide, feat_width = main.shape
    rows = 2 * wide + down.size // feat_width
    shape = jax.ShapeDtypeStruct((rows, feat_width), main.dtype)
    return local_call(pack_kernel, "pack_weights", 6, [VMEM, VMEM], [VMEM], [shape], after)(main, down)


def pair_kernel(which, place, ids_ref, own_ref, got_ref, out_ref, both_ref, sems):
    axis, shift = which
    bit = (ids_ref[axis] // shift) % 2
    lead = (slice(None),) * place
    copies = [
        pltpu.make_async_copy(own_ref, both_ref.at[lead + (bit,)], sems.at[0]),
        pltpu.make_async_copy(got_ref, both_ref.at[lead + (1 - bit,)], sems.at[1]),
    ]
    for copy in copies:
        copy.start()
    for copy in copies:
        copy.wait()
    whole = pltpu.make_async_copy(both_ref, out_ref, sems.at[2])
    whole.start()
    whole.wait()


def pair_up(ids, own, got, which, place, after):
    shape = own.shape[:place] + (2,) + own.shape[place:]
    return local_call(
        functools.partial(pair_kernel, which, place),
        "pair_up",
        8,
        [SMEM, ANY, ANY],
        [ANY],
        [jax.ShapeDtypeStruct(shape, own.dtype)],
        after,
        scratch=[pltpu.VMEM(shape, own.dtype), pltpu.SemaphoreType.DMA((3,))],
    )(ids, own, got)


AXES = ("page", "tok")


def some_lengths(length, bit, least):
    pages = lax.axis_size("page")
    lengths = jnp.where(jnp.arange(pages) == lax.axis_index("page"), length, 0)
    while bit > least:
        lengths = lengths + swap(lengths, "page", bit)
        bit //= 2
    return lengths


ORDER = (
    ("first",),
    ("lengths",),
    ("pack",),
    ("spread",),
    ("second", 0),
    ("wide", 0),
    ("second", 1),
    ("join", 0),
    ("after_two", 0),
    ("join", 1),
    ("wide", 1),
    ("forward", 0),
    ("join", 2),
    ("forward", 1),
    ("finish", 0),
    ("join", 3),
    ("forward", 2),
    ("finish", 1),
    ("forward", 3),
    ("after_weights",),
    ("finish", 2),
    ("finish", 3),
)


def packed_device(tile_tokens, page_lengths, occupancy, block_mix, stride_mix, w_gate_up, w_down):
    ids = jnp.stack([lax.axis_index("page"), lax.axis_index("tok")]).astype(jnp.int32)
    pages, parts = lax.axis_size("page"), lax.axis_size("tok")
    feat_width = tile_tokens.shape[2]
    spans = [feat_width * eighths // 8 for eighths in SPANS]
    tokens, held = [], {}

    def chained(name, step, *operands):
        results, token = step(*operands, (list(tokens), BRIEF))
        tokens[:] = [token]
        return results

    def plane(value):
        here = 2 * parts
        groups = [[level * here + i for i in range(here)] for level in range(pages // 2)]
        return lax.all_gather(value.reshape((-1,) + value.shape[2:]), AXES, axis_index_groups=groups)

    far_lengths = some_lengths(page_lengths[0], pages // 2, 1)
    lengths = far_lengths + swap(far_lengths, "page", 1)
    place = [ids, lengths]

    def swap_pages(k, own):
        held["own", k], held["got", k] = own, swap(own, "page", 1)

    def pack():
        value = chained("pack", pack_weights, jnp.swapaxes(w_gate_up, 1, 2), jnp.swapaxes(w_down, 0, 1))[0]
        held["weights"], held["across"] = value, swap(value, "page", 4)

    def first():
        groups = (spans[0], sum(spans[1:]))
        found = chained("first", first_factor, ids, page_lengths, occupancy, tile_tokens, block_mix, parts, groups)
        for k in range(2):
            mine = found[k * parts:(k + 1) * parts]
            held["first", k] = mine[:1] + [swap(mine[other], "tok", other) for other in range(1, parts)]

    def spread():
        held["spread"] = chained("spread", spread_stride, ids, stride_mix, parts)[0]

    def second(k):
        begin, here = (spans[0], spans[1:]) if k else (0, spans[:1])
        operands = (begin, here, *place, occupancy, held["spread"], held["first", k], tile_tokens)
        for i, own in enumerate(chained("second", second_factor, *operands)):
            swap_pages(k + i, own)

    def wide(k):
        value = chained("wide", pair_up, ids, held["weights"], held["across"], (0, 4 - 2 * k), k)[0]
        if k:
            held["weights"] = plane(value)
        else:
            held["weights"], held["across"] = value, swap(value, "page", 2)

    def join(k):
        value = chained("join", join_parity, *place, held["own", k], held["got", k])[0]
        held["one", k] = lax.ppermute(value, "page", [(4, 2), (5, 3), (6, 4), (7, 5), (2, 6), (3, 7)])
        held["two", k] = lax.ppermute(value, "page", [(6, 2), (7, 3), (2, 6), (3, 7)])
        held["own", k] = value

    def forward(k):
        value = chained("forward", forward_merge, *place, held["own", k], held["one", k], held["two", k])[0]
        held["last", k] = lax.ppermute(value, "page", [(2, 0), (3, 1), (0, 2), (1, 3)])

    def finish(k):
        found = [held[kind, k] for kind in ("own", "one", "two", "last")]
        held["source", k] = chained("finish", final_merge, *place, *found)[0]

    def lengths_first():
        tokens.append(far_lengths)

    def after_one(k):
        tokens.append(held["one", k])

    def after_two(k):
        tokens.append(held["two", k])

    def after_weights():
        tokens.append(held["weights"])

    steps = dict(pack=pack, first=first, spread=spread, second=second, wide=wide, join=join, forward=forward, finish=finish)
    steps.update(lengths=lengths_first, after_one=after_one, after_two=after_two, after_weights=after_weights)
    for name, *which in ORDER:
        steps[name](*which)
    return packed_mlp([held["source", k] for k in range(len(spans))], held["weights"])


def solution(mesh):
    pages, parts = mesh.shape["page"], mesh.shape["tok"]
    return jax.shard_map(
        packed_device if (pages, parts) == (8, 4) else per_device,
        mesh=mesh,
        in_specs=(
            P("page", "tok", None),
            P("page"),
            P("page", "tok"),
            P("tok", None, None),
            P("tok", None, None),
            P(None, None, ("page", "tok")),
            P(None, ("page", "tok")),
        ),
        out_specs=P("tok", "page", None),
        check_vma=False,
    )
```

```python
import functools

import jax
import jax.numpy as jnp
from jax import lax
from jax.experimental import pallas as pl
from jax.experimental.pallas import tpu as pltpu
from jax.sharding import PartitionSpec as P

epsilon = 1e-05


def entering(value, axis, join, neutral):
    count, mine = (lax.axis_size(axis), lax.axis_index(axis))
    pieces = lax.all_gather(value, axis)
    so_far = jnp.full_like(value, 0) + jnp.asarray(neutral, value.dtype)

    def hop(position, so_far):
        longer = join(so_far, pieces[position])
        return jnp.where(position < mine, longer, so_far)

    return lax.fori_loop(0, count - 1, hop, so_far)


def from_behind(value, axis, by):
    length = lax.axis_size(axis)
    pairs = [(i, i + by) for i in range(length) if 0 <= i + by < length]
    return lax.ppermute(value, axis, pairs)


def rms_round(values):
    scale = lax.rsqrt(jnp.mean(values * values, axis=-1, keepdims=True) + epsilon)
    return (values * scale).astype(jnp.bfloat16)


def add_counts(earlier, later):
    return earlier + later


def channel_mlp(mixed, w_gate_up, w_down):
    mixed_float = mixed.astype(jnp.float32)
    normed_two = rms_round(mixed_float)
    shard_part = lax.all_gather(w_gate_up, ("page", "tok"), axis=2, tiled=True)
    gate_vals = jnp.dot(normed_two, shard_part[0], preferred_element_type=jnp.float32)
    up_vals = jnp.dot(normed_two, shard_part[1], preferred_element_type=jnp.float32)
    hidden = (jax.nn.silu(gate_vals) * up_vals).astype(jnp.bfloat16)
    down_vals = jnp.dot(
        hidden,
        lax.all_gather(w_down, ("page", "tok"), axis=1, tiled=True),
        preferred_element_type=jnp.float32,
    )
    return (mixed_float + down_vals).astype(jnp.bfloat16)


def lane_relay(row_data, length, lane_index):
    row_count = row_data.shape[0]
    page_here = lax.axis_index("page")
    live_rows = jnp.clip(length - lane_index * row_count, 0, row_count)
    before = entering(live_rows.reshape(1), "page", add_counts, jnp.zeros((1,), jnp.int32))[0]
    distance = page_here * row_count - before
    in_shift = distance % row_count
    hop_count = distance // row_count
    row_ids = jnp.arange(row_count, dtype=jnp.int32)
    live_flag = row_ids < live_rows
    kept_data = jnp.where(live_flag[:, None], row_data, jnp.zeros_like(row_data))
    kept_tags = jnp.where(live_flag, hop_count + 1, 0).astype(jnp.int32)
    zero_data = jnp.zeros_like(row_data)
    zero_tags = jnp.zeros_like(kept_tags)
    here_data = lax.dynamic_slice_in_dim(
        jnp.concatenate([kept_data, zero_data], 0), in_shift, row_count, 0
    )
    here_tags = lax.dynamic_slice_in_dim(
        jnp.concatenate([kept_tags, zero_tags], 0), in_shift, row_count, 0
    )
    spill_data = lax.dynamic_slice_in_dim(
        jnp.concatenate([zero_data, kept_data], 0), in_shift, row_count, 0
    )
    spill_tags = lax.dynamic_slice_in_dim(
        jnp.concatenate([zero_tags, kept_tags], 0), in_shift, row_count, 0
    )
    got_data, got_tags = from_behind((spill_data, spill_tags), "page", -1)
    arrived = got_tags > 0
    cur_data = jnp.where(arrived[:, None], got_data, here_data)
    cur_tags = jnp.where(arrived, got_tags, here_tags)
    for bit_pos in range((lax.axis_size("page") - 1).bit_length()):
        stride_len = 1 << bit_pos
        present = cur_tags > 0
        moving = present & ((cur_tags - 1) // stride_len % 2 == 1)
        staying = present & jnp.logical_not(moving)
        out_data = jnp.where(moving[:, None], cur_data, jnp.zeros_like(cur_data))
        out_tags = jnp.where(moving, cur_tags, 0)
        got_data, got_tags = from_behind((out_data, out_tags), "page", -stride_len)
        arrived = got_tags > 0
        kept_now = jnp.where(staying[:, None], cur_data, jnp.zeros_like(cur_data))
        cur_data = jnp.where(arrived[:, None], got_data, kept_now)
        cur_tags = jnp.where(arrived, got_tags, jnp.where(staying, cur_tags, 0))
    return cur_data


def per_device(tile_tokens, page_lengths, occupancy, block_mix, stride_mix, w_gate_up, w_down):
    lane_index = lax.axis_index("tok")
    row_count = tile_tokens.shape[1]
    feat_width = tile_tokens.shape[2]
    blocks_here = block_mix.shape[0]
    blk_size = block_mix.shape[1]
    length = page_lengths[0]
    positions = lane_index * row_count + jnp.arange(row_count, dtype=jnp.int32)
    live_mask = (positions < length) & (jnp.repeat(occupancy[0], blk_size) > 0)
    masked = jnp.where(live_mask[:, None], tile_tokens[0].astype(jnp.float32), 0.0)
    normed = rms_round(masked).reshape(blocks_here, blk_size, feat_width)
    first = jnp.einsum(
        "bji,bic->bjc", block_mix, normed, preferred_element_type=jnp.float32
    ).astype(jnp.bfloat16)
    second = jnp.einsum(
        "jkb,bjc->jkc",
        stride_mix,
        lax.all_to_all(first, "tok", split_axis=1, concat_axis=0, tiled=True),
        preferred_element_type=jnp.float32,
    )
    mixed = (masked + second.reshape(row_count, feat_width)).astype(jnp.bfloat16)
    layer_out = channel_mlp(mixed, w_gate_up, w_down)
    packed = lane_relay(layer_out, length, lane_index)
    return packed.reshape(1, row_count, feat_width)


SMEM = pl.BlockSpec(memory_space=pltpu.SMEM)
VMEM = pl.BlockSpec(memory_space=pltpu.VMEM)
ANY = pl.BlockSpec(memory_space=pl.ANY)
MIB = 1024 * 1024
GROUP = 16
BLOCKS = 2
MLP_MIB = 30
SUB = 8
SPANS = (2, 2, 2, 2)
BRIEF = 1
TOKEN = jax.ShapeDtypeStruct((8, 128), jnp.int32)


def local_call(kernel, name, limit, in_specs, out_specs, out_shape, after, grid=(), scratch=()):
    after, cost = after
    ins, waits, outs = len(in_specs), len(after), len(out_specs)

    def body(*refs):
        token_ref = refs[ins + waits + outs]
        kernel(*refs[:ins], *refs[ins + waits:ins + waits + outs], *refs[ins + waits + outs + 1:])
        token_ref[...] = jnp.zeros(token_ref.shape, token_ref.dtype)

    token_spec = pl.BlockSpec(TOKEN.shape, lambda *_: (0, 0)) if grid else VMEM
    call = pl.pallas_call(
        body,
        grid=grid,
        in_specs=list(in_specs) + [ANY] * waits,
        out_specs=list(out_specs) + [token_spec],
        out_shape=list(out_shape) + [TOKEN],
        scratch_shapes=list(scratch),
        compiler_params=pltpu.CompilerParams(vmem_limit_bytes=limit * MIB),
        cost_estimate=pl.CostEstimate(flops=cost, bytes_accessed=cost // 1000, transcendentals=0),
        name=name,
    )

    def run(*operands):
        *results, token = call(*operands, *after)
        return results, token

    return run


def live_rows(start, shape, length, occupied):
    ids = start + lax.broadcasted_iota(jnp.int32, shape, 0)
    return (ids < length) & (occupied > 0)


def first_kernel(ids_ref, length_ref, occ_ref, tile_ref, mix_ref, *out_refs):
    step = pl.program_id(0)
    blocks, blk_size = mix_ref.shape[:2]
    feat_width = tile_ref.shape[2]
    lane = ids_ref[1]
    share = out_refs[0].shape[1]
    parts = blk_size // share
    rows_here = pl.num_programs(0) * blocks * blk_size
    for i in range(blocks):
        block = step * blocks + i
        start = lane * rows_here + block * blk_size
        live = live_rows(start, (blk_size, feat_width), length_ref[0], occ_ref[0, block])
        tile = tile_ref[0, i * blk_size:(i + 1) * blk_size, :]
        masked = jnp.where(live, tile.astype(jnp.float32), 0.0)
        normed = rms_round(masked)
        picked = [mix_ref[i, pl.ds(pl.multiple_of((lane ^ part) * share, share), share), :] for part in range(parts)]
        mix = jnp.concatenate(picked, axis=0)
        first = jnp.dot(mix, normed, preferred_element_type=jnp.float32).astype(jnp.bfloat16)
        begin = 0
        for group in range(len(out_refs) // parts):
            end = begin + out_refs[group * parts].shape[2]
            for part in range(parts):
                out_refs[group * parts + part][i] = first[part * share:(part + 1) * share, begin:end]
            begin = end


def first_factor(ids, length, occupancy, tile_tokens, block_mix, parts, groups, after):
    blocks, blk_size, _ = block_mix.shape
    feat_width = tile_tokens.shape[2]
    share = blk_size // parts
    each = 2
    return local_call(
        first_kernel,
        "first_factor",
        16,
        [
            SMEM,
            SMEM,
            SMEM,
            pl.BlockSpec((1, each * blk_size, feat_width), lambda b: (0, b, 0)),
            pl.BlockSpec((each, blk_size, blk_size), lambda b: (b, 0, 0)),
        ],
        [pl.BlockSpec((each, share, width), lambda b: (b, 0, 0)) for width in groups for _ in range(parts)],
        [jax.ShapeDtypeStruct((blocks, share, width), jnp.bfloat16) for width in groups for _ in range(parts)],
        after,
        grid=(blocks // each,),
    )(ids, length, occupancy, tile_tokens, block_mix)


def spread_kernel(parts, ids_ref, stride_ref, out_ref):
    spots, outs, ins = stride_ref.shape
    rows, cols = GROUP * outs, GROUP * ins
    column = lax.broadcasted_iota(jnp.int32, (ins, cols), 1) // GROUP
    here = ins // parts
    block = ((column // here) ^ ids_ref[1]) * here + column % here
    picks = block == lax.broadcasted_iota(jnp.int32, (ins, cols), 0)
    picks = picks.astype(jnp.float32).astype(jnp.bfloat16)
    spot_row = lax.broadcasted_iota(jnp.int32, (rows, cols), 0) // outs
    spot_col = lax.broadcasted_iota(jnp.int32, (rows, cols), 1) % GROUP
    for group in range(spots // GROUP):
        flat = stride_ref[group * GROUP:(group + 1) * GROUP].reshape(rows, ins)
        wide = jnp.dot(flat, picks, preferred_element_type=jnp.float32)
        out_ref[group] = jnp.where(spot_row == spot_col, wide, 0.0).astype(jnp.bfloat16)


def spread_stride(ids, stride_mix, parts, after):
    spots, outs, ins = stride_mix.shape
    shape = jax.ShapeDtypeStruct((spots // GROUP, GROUP * outs, GROUP * ins), jnp.bfloat16)
    kernel = functools.partial(spread_kernel, parts)
    return local_call(kernel, "spread_stride", 12, [SMEM, VMEM], [VMEM], [shape], after)(ids, stride_mix)


def kept_of(length, lane, rows):
    return jnp.clip(length - lane * rows, 0, rows)


def offset_of(lengths_ref, page, lane, rows):
    total = jnp.int32(0)
    for earlier in range(lengths_ref.shape[0]):
        total += jnp.where(earlier < page, kept_of(lengths_ref[earlier], lane, rows), 0)
    return total


def second_kernel(parts, begin, ids_ref, lengths_ref, occ_ref, spread_ref, *refs):
    first_refs, tile_ref, out_refs, twice_ref = refs[:parts], refs[parts], refs[parts + 1:-1], refs[-1]
    rows, width = tile_ref.shape[1], first_refs[0].shape[2]
    page, lane = ids_ref[0], ids_ref[1]
    length = lengths_ref[page]
    groups, group_rows, depth = spread_ref.shape
    blk_size = rows // occ_ref.shape[1]
    for group in range(groups):
        values = [ref[:, group * GROUP:(group + 1) * GROUP, :].reshape(depth // parts, width) for ref in first_refs]
        second = jnp.dot(spread_ref[group], jnp.concatenate(values, axis=0), preferred_element_type=jnp.float32)
        for part in range(group_rows // blk_size):
            at = group * group_rows + part * blk_size
            live = live_rows(lane * rows + at, (blk_size, width), length, occ_ref[0, at // blk_size])
            tile = tile_ref[0, at:at + blk_size, begin:begin + width]
            masked = jnp.where(live, tile.astype(jnp.float32), 0.0)
            mixed = masked + second[part * blk_size:(part + 1) * blk_size]
            mixed = mixed.astype(jnp.bfloat16).astype(jnp.float32)
            twice_ref[at:at + blk_size, :] = mixed
            twice_ref[rows + at:rows + at + blk_size, :] = mixed
    twice_ref[2 * rows:, :] = jnp.zeros((SUB, width), jnp.float32)
    start = rows - offset_of(lengths_ref, page, lane, rows) % rows
    extra = start % SUB
    base = pl.multiple_of(start - extra, SUB)
    tall = twice_ref[pl.ds(base, rows + SUB), :].reshape(rows // SUB + 1, SUB, width)
    tall = pltpu.roll(tall, (SUB - extra) % SUB, 1)
    inside = lax.broadcasted_iota(jnp.int32, (1, SUB, width), 1) + extra < SUB
    turned = jnp.where(inside, tall[:-1], tall[1:]).reshape(rows, width).astype(jnp.bfloat16)
    begin = 0
    for out_ref in out_refs:
        end = begin + out_ref.shape[1]
        out_ref[...] = turned[:, begin:end]
        begin = end


def second_factor(begin, spans, ids, lengths, occupancy, spread, firsts, tile_tokens, after):
    rows = tile_tokens.shape[1]
    width = firsts[0].shape[2]
    parts = len(firsts)
    return local_call(
        functools.partial(second_kernel, parts, begin),
        "second_factor",
        24,
        [SMEM, SMEM, SMEM, VMEM] + [VMEM] * parts + [VMEM],
        [VMEM] * len(spans),
        [jax.ShapeDtypeStruct((rows, span), jnp.bfloat16) for span in spans],
        after,
        scratch=[pltpu.VMEM((2 * rows + SUB, width), jnp.float32)],
    )(ids, lengths, occupancy, spread, *firsts, tile_tokens)


def pick(mask, yes_ref, no_ref):
    return jnp.where(mask, yes_ref[...].astype(jnp.float32), no_ref[...].astype(jnp.float32))


def parity_kernel(ids_ref, lengths_ref, own_ref, got_ref, out_ref):
    rows = own_ref.shape[0]
    page, lane = ids_ref[0], ids_ref[1]
    offset = offset_of(lengths_ref, page, lane, rows)
    kept = kept_of(lengths_ref[page], lane, rows)
    slot = lax.broadcasted_iota(jnp.int32, own_ref.shape, 0)
    base, shift = offset // rows, offset % rows
    early = (base % 2 == page % 2).astype(jnp.int32)
    low = jnp.where(early == 1, shift, 0)
    high = jnp.where(early == 1, jnp.minimum(shift + kept, rows), shift + kept - rows)
    out_ref[...] = pick((slot >= low) & (slot < high), own_ref, got_ref).astype(out_ref.dtype)


def join_parity(ids, lengths, own, got, after):
    shape = jax.ShapeDtypeStruct(own.shape, own.dtype)
    return local_call(parity_kernel, "join_parity", 6, [SMEM, SMEM, VMEM, VMEM], [VMEM], [shape], after)(ids, lengths, own, got)


def forward_kernel(ids_ref, lengths_ref, own_ref, one_ref, two_ref, out_ref):
    rows = own_ref.shape[0]
    page, lane = ids_ref[0], ids_ref[1]
    level = page // 2
    slot = (page % 2) * rows + lax.broadcasted_iota(jnp.int32, own_ref.shape, 0)
    after_one = offset_of(lengths_ref, 2 * level + 2, lane, rows)
    after_two = offset_of(lengths_ref, 2 * level + 4, lane, rows)
    value = pick(slot < after_two, one_ref, two_ref)
    out_ref[...] = jnp.where(slot < after_one, own_ref[...].astype(jnp.float32), value).astype(out_ref.dtype)


def forward_merge(ids, lengths, own, one, two, after):
    shape = jax.ShapeDtypeStruct(own.shape, own.dtype)
    specs = [SMEM, SMEM, VMEM, VMEM, VMEM]
    return local_call(forward_kernel, "forward_merge", 6, specs, [VMEM], [shape], after)(ids, lengths, own, one, two)


def final_kernel(ids_ref, lengths_ref, own_ref, one_ref, two_ref, last_ref, out_ref):
    rows = own_ref.shape[0]
    page, lane = ids_ref[0], ids_ref[1]
    level = page // 2
    slot = page * rows + lax.broadcasted_iota(jnp.int32, own_ref.shape, 0)
    ends = [offset_of(lengths_ref, 2 * (level + ahead), lane, rows) for ahead in (1, 2)]
    total = offset_of(lengths_ref, lengths_ref.shape[0], lane, rows)

    @pl.when(level == 0)
    def _():
        value = pick(slot < ends[0], own_ref, last_ref)
        out_ref[...] = jnp.where(slot < total, value, 0.0).astype(out_ref.dtype)

    @pl.when(level > 0)
    def _():
        value = pick(slot < ends[1], one_ref, two_ref)
        value = jnp.where(slot < ends[0], own_ref[...].astype(jnp.float32), value)
        out_ref[...] = jnp.where(slot < total, value, 0.0).astype(out_ref.dtype)


def final_merge(ids, lengths, own, one, two, last, after):
    shape = jax.ShapeDtypeStruct(own.shape, own.dtype)
    specs = [SMEM, SMEM, VMEM, VMEM, VMEM, VMEM]
    return local_call(final_kernel, "final_merge", 8, specs, [VMEM], [shape], after)(ids, lengths, own, one, two, last)


NT = (((1,), (1,)), ((), ()))


def mlp_kernel(pieces, ids_ref, *refs):
    sources, refs = refs[:pieces], refs[pieces:]
    own_gate, got_gate, own_up, got_up, out_ref = refs
    core = ids_ref[1] % 2

    @pl.when(core == 0)
    def _():
        mlp_rows(sources, (own_gate, got_gate), (own_up, got_up), out_ref)

    @pl.when(core == 1)
    def _():
        mlp_rows(sources, (got_gate, own_gate), (got_up, own_up), out_ref)


def mlp_rows(sources, gate_refs, up_refs, out_ref):
    here, levels, each, feat_width = gate_refs[0].shape
    thin = feat_width // (2 * here * levels)
    wide = each - thin
    rows = out_ref.shape[1]
    block = rows // BLOCKS

    def weights(refs, level, rows):
        return jnp.concatenate([ref[i, level, rows, :] for i in range(here) for ref in refs], axis=0)

    def times(values, matrix):
        return lax.dot_general(values, matrix, NT, preferred_element_type=jnp.float32)

    for at in range(0, rows, block):
        mixed = jnp.concatenate([ref[at:at + block, :] for ref in sources], axis=1).astype(jnp.float32)
        normed = rms_round(mixed)
        hidden = []
        for level in range(levels):
            gate = times(normed, weights(gate_refs, level, slice(0, wide)))
            up = times(normed, weights(up_refs, level, slice(0, wide)))
            hidden.append((gate / (1.0 + jnp.exp(-gate)) * up).astype(jnp.bfloat16))
        hidden = jnp.concatenate(hidden, axis=1)
        for level in range(levels):
            cols = slice(level * 2 * here * thin, (level + 1) * 2 * here * thin)
            result = mixed[:, cols]
            for part, found in enumerate((gate_refs, up_refs)):
                inner = hidden[:, part * feat_width:(part + 1) * feat_width]
                result += times(inner, weights(found, level, slice(wide, each)))
            out_ref[0, at:at + block, cols] = result.astype(out_ref.dtype)


def packed_mlp(ids, sources, weights):
    rows, feat_width = sources[0].shape[0], weights[0].shape[3]
    return pl.pallas_call(
        functools.partial(mlp_kernel, len(sources)),
        in_specs=[SMEM] + [VMEM] * (len(sources) + 4),
        out_specs=VMEM,
        out_shape=jax.ShapeDtypeStruct((1, rows, feat_width), jnp.bfloat16),
        compiler_params=pltpu.CompilerParams(vmem_limit_bytes=MLP_MIB * MIB),
        name="packed_mlp",
    )(ids, *sources, *weights)


def swap(value, axis, bit):
    return lax.ppermute(value, axis, [(i, i ^ bit) for i in range(lax.axis_size(axis))])


def pack_kernel(main_ref, down_ref, *out_refs):
    wide, feat_width = main_ref.shape[1:]
    for part, out_ref in enumerate(out_refs):
        out_ref[:wide] = main_ref[part]
        out_ref[wide:] = down_ref[:, part * feat_width:(part + 1) * feat_width]


def pack_weights(main, down, after):
    _, wide, feat_width = main.shape
    thin = down.shape[0]
    shape = jax.ShapeDtypeStruct((2 * (wide + thin), feat_width), main.dtype)
    return local_call(pack_both, "pack_weights", 6, [VMEM, VMEM], [VMEM], [shape], after)(main, down)


def pack_both(main_ref, down_ref, out_ref):
    rows = out_ref.shape[0] // 2
    pack_kernel(main_ref, down_ref, out_ref.at[:rows], out_ref.at[rows:])


def pair_kernel(which, place, ids_ref, own_ref, got_ref, out_ref, both_ref, sems):
    axis, shift = which
    bit = (ids_ref[axis] // shift) % 2
    lead = (slice(None),) * place
    copies = [
        pltpu.make_async_copy(own_ref, both_ref.at[lead + (bit,)], sems.at[0]),
        pltpu.make_async_copy(got_ref, both_ref.at[lead + (1 - bit,)], sems.at[1]),
    ]
    for copy in copies:
        copy.start()
    for copy in copies:
        copy.wait()
    whole = pltpu.make_async_copy(both_ref, out_ref, sems.at[2])
    whole.start()
    whole.wait()


def pair_up(ids, own, got, which, place, after):
    shape = own.shape[:place] + (2,) + own.shape[place:]
    return local_call(
        functools.partial(pair_kernel, which, place),
        "pair_up",
        8,
        [SMEM, ANY, ANY],
        [ANY],
        [jax.ShapeDtypeStruct(shape, own.dtype)],
        after,
        scratch=[pltpu.VMEM(shape, own.dtype), pltpu.SemaphoreType.DMA((3,))],
    )(ids, own, got)


AXES = ("page", "tok")


def some_lengths(length, bit, least):
    pages = lax.axis_size("page")
    lengths = jnp.where(jnp.arange(pages) == lax.axis_index("page"), length, 0)
    while bit > least:
        lengths = lengths + swap(lengths, "page", bit)
        bit //= 2
    return lengths


ORDER = (
    ("first",),
    ("lengths",),
    ("pack",),
    ("spread",),
    ("second", 0),
    ("wide", 0),
    ("second", 1),
    ("join", 0),
    ("after_two", 0),
    ("join", 1),
    ("wide", 1),
    ("join", 2),
    ("join", 3),
    ("forward", 0),
    ("forward", 1),
    ("broad", "gate", 0),
    ("broad", "up", 0),
    ("finish", 0),
    ("forward", 2),
    ("finish", 1),
    ("after_last", 2),
    ("forward", 3),
    ("broad", "gate", 1),
    ("broad", "up", 1),
    ("finish", 2),
    ("finish", 3),
)


def packed_device(tile_tokens, page_lengths, occupancy, block_mix, stride_mix, w_gate_up, w_down):
    ids = jnp.stack([lax.axis_index("page"), lax.axis_index("tok")]).astype(jnp.int32)
    pages, parts = lax.axis_size("page"), lax.axis_size("tok")
    feat_width = tile_tokens.shape[2]
    spans = [feat_width * eighths // 8 for eighths in SPANS]
    tokens, held = [], {}

    def chained(name, step, *operands):
        results, token = step(*operands, (list(tokens), BRIEF))
        tokens[:] = [token]
        return results

    def plane(value):
        here = 2 * parts
        groups = [[level * here + i for i in range(here)] for level in range(pages // 2)]
        return lax.all_gather(value.reshape((-1,) + value.shape[2:]), AXES, axis_index_groups=groups)

    far_lengths = some_lengths(page_lengths[0], pages // 2, 1)
    lengths = far_lengths + swap(far_lengths, "page", 1)
    place = [ids, lengths]

    def swap_pages(k, own):
        held["own", k], held["got", k] = own, swap(own, "page", 1)

    def pack():
        value = chained("pack", pack_weights, jnp.swapaxes(w_gate_up, 1, 2), jnp.swapaxes(w_down, 0, 1))[0]
        held["weights"], held["across"] = value, swap(value, "page", 4)

    def first():
        groups = (spans[0], sum(spans[1:]))
        found = chained("first", first_factor, ids, page_lengths, occupancy, tile_tokens, block_mix, parts, groups)
        for k in range(2):
            mine = found[k * parts:(k + 1) * parts]
            held["first", k] = mine[:1] + [swap(mine[other], "tok", other) for other in range(1, parts)]

    def spread():
        held["spread"] = chained("spread", spread_stride, ids, stride_mix, parts)[0]

    def second(k):
        begin, here = (spans[0], spans[1:]) if k else (0, spans[:1])
        operands = (begin, here, *place, occupancy, held["spread"], held["first", k], tile_tokens)
        for i, own in enumerate(chained("second", second_factor, *operands)):
            swap_pages(k + i, own)

    def paired(value, got, which, place):
        return chained("wide", pair_up, ids, value, got, which, place)[0]

    def wide(k):
        value = paired(held["weights"], held["across"], (0, 4 - 2 * k), k)
        held["weights"] = value
        if k == 0:
            held["across"] = swap(value, "page", 2)
        else:
            value = value.reshape((-1,) + value.shape[2:])
            cut = value.shape[1] // 2
            held["gate"], held["up"] = value[:, :cut], value[:, cut:]
            held["gate_got"], held["up_got"] = swap(held["gate"], "tok", 2), swap(held["up"], "page", 1)

    def broad(kind, k):
        bits = ((1, 2), (0, 1))
        y_first = kind == "gate"
        which = bits[k] if y_first else bits[1 - k]
        value = paired(held[kind], held[kind + "_got"], which, 0 if y_first or k == 0 else 1)
        if k == 0:
            next_axis = ("page", 1) if y_first else ("tok", 2)
            held[kind], held[kind + "_got"] = value, swap(value, *next_axis)
        else:
            value = value.reshape((-1,) + value.shape[2:])
            held[kind], held[kind + "_got"] = value, swap(value, "tok", 1)

    def join(k):
        value = chained("join", join_parity, *place, held["own", k], held["got", k])[0]
        held["one", k] = lax.ppermute(value, "page", [(4, 2), (5, 3), (6, 4), (7, 5), (2, 6), (3, 7)])
        held["two", k] = lax.ppermute(value, "page", [(6, 2), (7, 3), (2, 6), (3, 7)])
        held["own", k] = value

    def forward(k):
        value = chained("forward", forward_merge, *place, held["own", k], held["one", k], held["two", k])[0]
        held["last", k] = lax.ppermute(value, "page", [(2, 0), (3, 1), (0, 2), (1, 3)])

    def finish(k):
        found = [held[kind, k] for kind in ("own", "one", "two", "last")]
        held["source", k] = chained("finish", final_merge, *place, *found)[0]

    def lengths_first():
        tokens.append(far_lengths)

    def after_one(k):
        tokens.append(held["one", k])

    def after_two(k):
        tokens.append(held["two", k])

    def after_last(k):
        tokens.append(held["last", k])

    steps = dict(pack=pack, first=first, spread=spread, second=second, wide=wide, broad=broad)
    steps.update(join=join, forward=forward, finish=finish, lengths=lengths_first)
    steps.update(after_one=after_one, after_two=after_two, after_last=after_last)
    for name, *which in ORDER:
        steps[name](*which)
    weights = [held[kind] for kind in ("gate", "gate_got", "up", "up_got")]
    return packed_mlp(ids, [held["source", k] for k in range(len(spans))], weights)


def solution(mesh):
    pages, parts = mesh.shape["page"], mesh.shape["tok"]
    return jax.shard_map(
        packed_device if (pages, parts) == (8, 4) else per_device,
        mesh=mesh,
        in_specs=(
            P("page", "tok", None),
            P("page"),
            P("page", "tok"),
            P("tok", None, None),
            P("tok", None, None),
            P(None, None, ("page", "tok")),
            P(None, ("page", "tok")),
        ),
        out_specs=P("tok", "page", None),
        check_vma=False,
    )
```

```python
import functools

import jax
import jax.numpy as jnp
from jax import lax
from jax.experimental import pallas as pl
from jax.experimental.pallas import tpu as pltpu
from jax.sharding import PartitionSpec as P

epsilon = 1e-05


def entering(value, axis, join, neutral):
    count, mine = (lax.axis_size(axis), lax.axis_index(axis))
    pieces = lax.all_gather(value, axis)
    so_far = jnp.full_like(value, 0) + jnp.asarray(neutral, value.dtype)

    def hop(position, so_far):
        longer = join(so_far, pieces[position])
        return jnp.where(position < mine, longer, so_far)

    return lax.fori_loop(0, count - 1, hop, so_far)


def from_behind(value, axis, by):
    length = lax.axis_size(axis)
    pairs = [(i, i + by) for i in range(length) if 0 <= i + by < length]
    return lax.ppermute(value, axis, pairs)


def rms_round(values):
    scale = lax.rsqrt(jnp.mean(values * values, axis=-1, keepdims=True) + epsilon)
    return (values * scale).astype(jnp.bfloat16)


def add_counts(earlier, later):
    return earlier + later


def channel_mlp(mixed, w_gate_up, w_down):
    mixed_float = mixed.astype(jnp.float32)
    normed_two = rms_round(mixed_float)
    shard_part = lax.all_gather(w_gate_up, ("page", "tok"), axis=2, tiled=True)
    gate_vals = jnp.dot(normed_two, shard_part[0], preferred_element_type=jnp.float32)
    up_vals = jnp.dot(normed_two, shard_part[1], preferred_element_type=jnp.float32)
    hidden = (jax.nn.silu(gate_vals) * up_vals).astype(jnp.bfloat16)
    down_vals = jnp.dot(
        hidden,
        lax.all_gather(w_down, ("page", "tok"), axis=1, tiled=True),
        preferred_element_type=jnp.float32,
    )
    return (mixed_float + down_vals).astype(jnp.bfloat16)


def lane_relay(row_data, length, lane_index):
    row_count = row_data.shape[0]
    page_here = lax.axis_index("page")
    live_rows = jnp.clip(length - lane_index * row_count, 0, row_count)
    before = entering(live_rows.reshape(1), "page", add_counts, jnp.zeros((1,), jnp.int32))[0]
    distance = page_here * row_count - before
    in_shift = distance % row_count
    hop_count = distance // row_count
    row_ids = jnp.arange(row_count, dtype=jnp.int32)
    live_flag = row_ids < live_rows
    kept_data = jnp.where(live_flag[:, None], row_data, jnp.zeros_like(row_data))
    kept_tags = jnp.where(live_flag, hop_count + 1, 0).astype(jnp.int32)
    zero_data = jnp.zeros_like(row_data)
    zero_tags = jnp.zeros_like(kept_tags)
    here_data = lax.dynamic_slice_in_dim(
        jnp.concatenate([kept_data, zero_data], 0), in_shift, row_count, 0
    )
    here_tags = lax.dynamic_slice_in_dim(
        jnp.concatenate([kept_tags, zero_tags], 0), in_shift, row_count, 0
    )
    spill_data = lax.dynamic_slice_in_dim(
        jnp.concatenate([zero_data, kept_data], 0), in_shift, row_count, 0
    )
    spill_tags = lax.dynamic_slice_in_dim(
        jnp.concatenate([zero_tags, kept_tags], 0), in_shift, row_count, 0
    )
    got_data, got_tags = from_behind((spill_data, spill_tags), "page", -1)
    arrived = got_tags > 0
    cur_data = jnp.where(arrived[:, None], got_data, here_data)
    cur_tags = jnp.where(arrived, got_tags, here_tags)
    for bit_pos in range((lax.axis_size("page") - 1).bit_length()):
        stride_len = 1 << bit_pos
        present = cur_tags > 0
        moving = present & ((cur_tags - 1) // stride_len % 2 == 1)
        staying = present & jnp.logical_not(moving)
        out_data = jnp.where(moving[:, None], cur_data, jnp.zeros_like(cur_data))
        out_tags = jnp.where(moving, cur_tags, 0)
        got_data, got_tags = from_behind((out_data, out_tags), "page", -stride_len)
        arrived = got_tags > 0
        kept_now = jnp.where(staying[:, None], cur_data, jnp.zeros_like(cur_data))
        cur_data = jnp.where(arrived[:, None], got_data, kept_now)
        cur_tags = jnp.where(arrived, got_tags, jnp.where(staying, cur_tags, 0))
    return cur_data


def per_device(tile_tokens, page_lengths, occupancy, block_mix, stride_mix, w_gate_up, w_down):
    lane_index = lax.axis_index("tok")
    row_count = tile_tokens.shape[1]
    feat_width = tile_tokens.shape[2]
    blocks_here = block_mix.shape[0]
    blk_size = block_mix.shape[1]
    length = page_lengths[0]
    positions = lane_index * row_count + jnp.arange(row_count, dtype=jnp.int32)
    live_mask = (positions < length) & (jnp.repeat(occupancy[0], blk_size) > 0)
    masked = jnp.where(live_mask[:, None], tile_tokens[0].astype(jnp.float32), 0.0)
    normed = rms_round(masked).reshape(blocks_here, blk_size, feat_width)
    first = jnp.einsum(
        "bji,bic->bjc", block_mix, normed, preferred_element_type=jnp.float32
    ).astype(jnp.bfloat16)
    second = jnp.einsum(
        "jkb,bjc->jkc",
        stride_mix,
        lax.all_to_all(first, "tok", split_axis=1, concat_axis=0, tiled=True),
        preferred_element_type=jnp.float32,
    )
    mixed = (masked + second.reshape(row_count, feat_width)).astype(jnp.bfloat16)
    layer_out = channel_mlp(mixed, w_gate_up, w_down)
    packed = lane_relay(layer_out, length, lane_index)
    return packed.reshape(1, row_count, feat_width)


SMEM = pl.BlockSpec(memory_space=pltpu.SMEM)
VMEM = pl.BlockSpec(memory_space=pltpu.VMEM)
ANY = pl.BlockSpec(memory_space=pl.ANY)
MIB = 1024 * 1024
GROUP = 16
BLOCKS = 2
MLP_MIB = 30
SUB = 8
SPANS = (2, 2, 2, 2)
BRIEF = 1
TOKEN = jax.ShapeDtypeStruct((8, 128), jnp.int32)


def local_call(kernel, name, limit, in_specs, out_specs, out_shape, after, grid=(), scratch=()):
    after, cost = after
    ins, waits, outs = len(in_specs), len(after), len(out_specs)

    def body(*refs):
        token_ref = refs[ins + waits + outs]
        kernel(*refs[:ins], *refs[ins + waits:ins + waits + outs], *refs[ins + waits + outs + 1:])
        token_ref[...] = jnp.zeros(token_ref.shape, token_ref.dtype)

    token_spec = pl.BlockSpec(TOKEN.shape, lambda *_: (0, 0)) if grid else VMEM
    call = pl.pallas_call(
        body,
        grid=grid,
        in_specs=list(in_specs) + [ANY] * waits,
        out_specs=list(out_specs) + [token_spec],
        out_shape=list(out_shape) + [TOKEN],
        scratch_shapes=list(scratch),
        compiler_params=pltpu.CompilerParams(vmem_limit_bytes=limit * MIB),
        cost_estimate=pl.CostEstimate(flops=cost, bytes_accessed=cost // 1000, transcendentals=0),
        name=name,
    )

    def run(*operands):
        *results, token = call(*operands, *after)
        return results, token

    return run


def live_rows(start, shape, length, occupied):
    ids = start + lax.broadcasted_iota(jnp.int32, shape, 0)
    return (ids < length) & (occupied > 0)


def first_kernel(ids_ref, length_ref, occ_ref, tile_ref, mix_ref, *out_refs):
    step = pl.program_id(0)
    blocks, blk_size = mix_ref.shape[:2]
    feat_width = tile_ref.shape[2]
    lane = ids_ref[1]
    share = out_refs[0].shape[1]
    parts = blk_size // share
    rows_here = pl.num_programs(0) * blocks * blk_size
    for i in range(blocks):
        block = step * blocks + i
        start = lane * rows_here + block * blk_size
        live = live_rows(start, (blk_size, feat_width), length_ref[0], occ_ref[0, block])
        tile = tile_ref[0, i * blk_size:(i + 1) * blk_size, :]
        masked = jnp.where(live, tile.astype(jnp.float32), 0.0)
        normed = rms_round(masked)
        picked = [mix_ref[i, pl.ds(pl.multiple_of((lane ^ part) * share, share), share), :] for part in range(parts)]
        mix = jnp.concatenate(picked, axis=0)
        first = jnp.dot(mix, normed, preferred_element_type=jnp.float32).astype(jnp.bfloat16)
        begin = 0
        for group in range(len(out_refs) // parts):
            end = begin + out_refs[group * parts].shape[2]
            for part in range(parts):
                out_refs[group * parts + part][i] = first[part * share:(part + 1) * share, begin:end]
            begin = end


def first_factor(ids, length, occupancy, tile_tokens, block_mix, parts, groups, after):
    blocks, blk_size, _ = block_mix.shape
    feat_width = tile_tokens.shape[2]
    share = blk_size // parts
    each = 2
    return local_call(
        first_kernel,
        "first_factor",
        16,
        [
            SMEM,
            SMEM,
            SMEM,
            pl.BlockSpec((1, each * blk_size, feat_width), lambda b: (0, b, 0)),
            pl.BlockSpec((each, blk_size, blk_size), lambda b: (b, 0, 0)),
        ],
        [pl.BlockSpec((each, share, width), lambda b: (b, 0, 0)) for width in groups for _ in range(parts)],
        [jax.ShapeDtypeStruct((blocks, share, width), jnp.bfloat16) for width in groups for _ in range(parts)],
        after,
        grid=(blocks // each,),
    )(ids, length, occupancy, tile_tokens, block_mix)


def spread_kernel(parts, ids_ref, stride_ref, out_ref):
    spots, outs, ins = stride_ref.shape
    rows, cols = GROUP * outs, GROUP * ins
    column = lax.broadcasted_iota(jnp.int32, (ins, cols), 1) // GROUP
    here = ins // parts
    block = ((column // here) ^ ids_ref[1]) * here + column % here
    picks = block == lax.broadcasted_iota(jnp.int32, (ins, cols), 0)
    picks = picks.astype(jnp.float32).astype(jnp.bfloat16)
    spot_row = lax.broadcasted_iota(jnp.int32, (rows, cols), 0) // outs
    spot_col = lax.broadcasted_iota(jnp.int32, (rows, cols), 1) % GROUP
    for group in range(spots // GROUP):
        flat = stride_ref[group * GROUP:(group + 1) * GROUP].reshape(rows, ins)
        wide = jnp.dot(flat, picks, preferred_element_type=jnp.float32)
        out_ref[group] = jnp.where(spot_row == spot_col, wide, 0.0).astype(jnp.bfloat16)


def spread_stride(ids, stride_mix, parts, after):
    spots, outs, ins = stride_mix.shape
    shape = jax.ShapeDtypeStruct((spots // GROUP, GROUP * outs, GROUP * ins), jnp.bfloat16)
    kernel = functools.partial(spread_kernel, parts)
    return local_call(kernel, "spread_stride", 12, [SMEM, VMEM], [VMEM], [shape], after)(ids, stride_mix)


def kept_of(length, lane, rows):
    return jnp.clip(length - lane * rows, 0, rows)


def offset_of(lengths_ref, page, lane, rows):
    total = jnp.int32(0)
    for earlier in range(lengths_ref.shape[0]):
        total += jnp.where(earlier < page, kept_of(lengths_ref[earlier], lane, rows), 0)
    return total


def second_kernel(parts, begin, ids_ref, lengths_ref, occ_ref, spread_ref, *refs):
    first_refs, tile_ref, out_refs, twice_ref = refs[:parts], refs[parts], refs[parts + 1:-1], refs[-1]
    rows, width = tile_ref.shape[1], first_refs[0].shape[2]
    page, lane = ids_ref[0], ids_ref[1]
    length = lengths_ref[page]
    groups, group_rows, depth = spread_ref.shape
    blk_size = rows // occ_ref.shape[1]
    for group in range(groups):
        values = [ref[:, group * GROUP:(group + 1) * GROUP, :].reshape(depth // parts, width) for ref in first_refs]
        second = jnp.dot(spread_ref[group], jnp.concatenate(values, axis=0), preferred_element_type=jnp.float32)
        for part in range(group_rows // blk_size):
            at = group * group_rows + part * blk_size
            live = live_rows(lane * rows + at, (blk_size, width), length, occ_ref[0, at // blk_size])
            tile = tile_ref[0, at:at + blk_size, begin:begin + width]
            masked = jnp.where(live, tile.astype(jnp.float32), 0.0)
            mixed = masked + second[part * blk_size:(part + 1) * blk_size]
            mixed = mixed.astype(jnp.bfloat16).astype(jnp.float32)
            twice_ref[at:at + blk_size, :] = mixed
            twice_ref[rows + at:rows + at + blk_size, :] = mixed
    twice_ref[2 * rows:, :] = jnp.zeros((SUB, width), jnp.float32)
    start = rows - offset_of(lengths_ref, page, lane, rows) % rows
    extra = start % SUB
    base = pl.multiple_of(start - extra, SUB)
    tall = twice_ref[pl.ds(base, rows + SUB), :].reshape(rows // SUB + 1, SUB, width)
    tall = pltpu.roll(tall, (SUB - extra) % SUB, 1)
    inside = lax.broadcasted_iota(jnp.int32, (1, SUB, width), 1) + extra < SUB
    turned = jnp.where(inside, tall[:-1], tall[1:]).reshape(rows, width).astype(jnp.bfloat16)
    begin = 0
    for out_ref in out_refs:
        end = begin + out_ref.shape[1]
        out_ref[...] = turned[:, begin:end]
        begin = end


def second_factor(begin, spans, ids, lengths, occupancy, spread, firsts, tile_tokens, after):
    rows = tile_tokens.shape[1]
    width = firsts[0].shape[2]
    parts = len(firsts)
    return local_call(
        functools.partial(second_kernel, parts, begin),
        "second_factor",
        24,
        [SMEM, SMEM, SMEM, VMEM] + [VMEM] * parts + [VMEM],
        [VMEM] * len(spans),
        [jax.ShapeDtypeStruct((rows, span), jnp.bfloat16) for span in spans],
        after,
        scratch=[pltpu.VMEM((2 * rows + SUB, width), jnp.float32)],
    )(ids, lengths, occupancy, spread, *firsts, tile_tokens)


def pick(mask, yes_ref, no_ref):
    return jnp.where(mask, yes_ref[...].astype(jnp.float32), no_ref[...].astype(jnp.float32))


def parity_kernel(ids_ref, lengths_ref, own_ref, got_ref, out_ref):
    rows = own_ref.shape[0]
    page, lane = ids_ref[0], ids_ref[1]
    offset = offset_of(lengths_ref, page, lane, rows)
    kept = kept_of(lengths_ref[page], lane, rows)
    slot = lax.broadcasted_iota(jnp.int32, own_ref.shape, 0)
    base, shift = offset // rows, offset % rows
    early = (base % 2 == page % 2).astype(jnp.int32)
    low = jnp.where(early == 1, shift, 0)
    high = jnp.where(early == 1, jnp.minimum(shift + kept, rows), shift + kept - rows)
    out_ref[...] = pick((slot >= low) & (slot < high), own_ref, got_ref).astype(out_ref.dtype)


def join_parity(ids, lengths, own, got, after):
    shape = jax.ShapeDtypeStruct(own.shape, own.dtype)
    return local_call(parity_kernel, "join_parity", 6, [SMEM, SMEM, VMEM, VMEM], [VMEM], [shape], after)(ids, lengths, own, got)


def forward_kernel(ids_ref, lengths_ref, own_ref, one_ref, two_ref, out_ref):
    rows = own_ref.shape[0]
    page, lane = ids_ref[0], ids_ref[1]
    level = page // 2
    slot = (page % 2) * rows + lax.broadcasted_iota(jnp.int32, own_ref.shape, 0)
    after_one = offset_of(lengths_ref, 2 * level + 2, lane, rows)
    after_two = offset_of(lengths_ref, 2 * level + 4, lane, rows)
    value = pick(slot < after_two, one_ref, two_ref)
    out_ref[...] = jnp.where(slot < after_one, own_ref[...].astype(jnp.float32), value).astype(out_ref.dtype)


def forward_merge(ids, lengths, own, one, two, after):
    shape = jax.ShapeDtypeStruct(own.shape, own.dtype)
    specs = [SMEM, SMEM, VMEM, VMEM, VMEM]
    return local_call(forward_kernel, "forward_merge", 6, specs, [VMEM], [shape], after)(ids, lengths, own, one, two)


def final_kernel(ids_ref, lengths_ref, own_ref, one_ref, two_ref, last_ref, out_ref):
    rows = own_ref.shape[0]
    page, lane = ids_ref[0], ids_ref[1]
    level = page // 2
    slot = page * rows + lax.broadcasted_iota(jnp.int32, own_ref.shape, 0)
    ends = [offset_of(lengths_ref, 2 * (level + ahead), lane, rows) for ahead in (1, 2)]
    total = offset_of(lengths_ref, lengths_ref.shape[0], lane, rows)

    @pl.when(level == 0)
    def _():
        value = pick(slot < ends[0], own_ref, last_ref)
        out_ref[...] = jnp.where(slot < total, value, 0.0).astype(out_ref.dtype)

    @pl.when(level > 0)
    def _():
        value = pick(slot < ends[1], one_ref, two_ref)
        value = jnp.where(slot < ends[0], own_ref[...].astype(jnp.float32), value)
        out_ref[...] = jnp.where(slot < total, value, 0.0).astype(out_ref.dtype)


def final_merge(ids, lengths, own, one, two, last, after):
    shape = jax.ShapeDtypeStruct(own.shape, own.dtype)
    specs = [SMEM, SMEM, VMEM, VMEM, VMEM, VMEM]
    return local_call(final_kernel, "final_merge", 8, specs, [VMEM], [shape], after)(ids, lengths, own, one, two, last)


NT = (((1,), (1,)), ((), ()))


def mlp_kernel(pieces, ids_ref, *refs):
    sources, refs = refs[:pieces], refs[pieces:]
    own_gate, got_gate, own_up, got_up, out_ref = refs
    core = ids_ref[1] % 2

    @pl.when(core == 0)
    def _():
        mlp_rows(sources, (own_gate, got_gate), (own_up, got_up), out_ref)

    @pl.when(core == 1)
    def _():
        mlp_rows(sources, (got_gate, own_gate), (got_up, own_up), out_ref)


def mlp_rows(sources, gate_refs, up_refs, out_ref):
    here, levels, each, feat_width = gate_refs[0].shape
    thin = feat_width // (2 * here * levels)
    wide = each - thin
    rows = out_ref.shape[1]
    block = rows // BLOCKS

    def weights(refs, level, rows):
        return jnp.concatenate([ref[i, level, rows, :] for i in range(here) for ref in refs], axis=0)

    def times(values, matrix):
        return lax.dot_general(values, matrix, NT, preferred_element_type=jnp.float32)

    for at in range(0, rows, block):
        mixed = jnp.concatenate([ref[at:at + block, :] for ref in sources], axis=1).astype(jnp.float32)
        normed = rms_round(mixed)
        hidden = []
        for level in range(levels):
            gate = times(normed, weights(gate_refs, level, slice(0, wide)))
            up = times(normed, weights(up_refs, level, slice(0, wide)))
            hidden.append((gate / (1.0 + jnp.exp(-gate)) * up).astype(jnp.bfloat16))
        hidden = jnp.concatenate(hidden, axis=1)
        for level in range(levels):
            cols = slice(level * 2 * here * thin, (level + 1) * 2 * here * thin)
            result = mixed[:, cols]
            for part, found in enumerate((gate_refs, up_refs)):
                inner = hidden[:, part * feat_width:(part + 1) * feat_width]
                result += times(inner, weights(found, level, slice(wide, each)))
            out_ref[0, at:at + block, cols] = result.astype(out_ref.dtype)


def packed_mlp(ids, sources, weights):
    rows, feat_width = sources[0].shape[0], weights[0].shape[3]
    return pl.pallas_call(
        functools.partial(mlp_kernel, len(sources)),
        in_specs=[SMEM] + [VMEM] * (len(sources) + 4),
        out_specs=VMEM,
        out_shape=jax.ShapeDtypeStruct((1, rows, feat_width), jnp.bfloat16),
        compiler_params=pltpu.CompilerParams(vmem_limit_bytes=MLP_MIB * MIB),
        name="packed_mlp",
    )(ids, *sources, *weights)


def swap(value, axis, bit):
    return lax.ppermute(value, axis, [(i, i ^ bit) for i in range(lax.axis_size(axis))])


def pack_kernel(main_ref, down_ref, *out_refs):
    wide, feat_width = main_ref.shape[1:]
    for part, out_ref in enumerate(out_refs):
        out_ref[:wide] = main_ref[part]
        out_ref[wide:] = down_ref[:, part * feat_width:(part + 1) * feat_width]


def pack_weights(main, down, after):
    _, wide, feat_width = main.shape
    thin = down.shape[0]
    shape = jax.ShapeDtypeStruct((2 * (wide + thin), feat_width), main.dtype)
    return local_call(pack_both, "pack_weights", 6, [VMEM, VMEM], [VMEM], [shape], after)(main, down)


def pack_both(main_ref, down_ref, out_ref):
    rows = out_ref.shape[0] // 2
    pack_kernel(main_ref, down_ref, out_ref.at[:rows], out_ref.at[rows:])


def pair_kernel(which, place, ids_ref, own_ref, got_ref, out_ref, both_ref, sems):
    axis, shift = which
    bit = (ids_ref[axis] // shift) % 2
    lead = (slice(None),) * place
    copies = [
        pltpu.make_async_copy(own_ref, both_ref.at[lead + (bit,)], sems.at[0]),
        pltpu.make_async_copy(got_ref, both_ref.at[lead + (1 - bit,)], sems.at[1]),
    ]
    for copy in copies:
        copy.start()
    for copy in copies:
        copy.wait()
    whole = pltpu.make_async_copy(both_ref, out_ref, sems.at[2])
    whole.start()
    whole.wait()


def pair_up(ids, own, got, which, place, after):
    shape = own.shape[:place] + (2,) + own.shape[place:]
    return local_call(
        functools.partial(pair_kernel, which, place),
        "pair_up",
        8,
        [SMEM, ANY, ANY],
        [ANY],
        [jax.ShapeDtypeStruct(shape, own.dtype)],
        after,
        scratch=[pltpu.VMEM(shape, own.dtype), pltpu.SemaphoreType.DMA((3,))],
    )(ids, own, got)


AXES = ("page", "tok")


def some_lengths(length, bit, least):
    pages = lax.axis_size("page")
    lengths = jnp.where(jnp.arange(pages) == lax.axis_index("page"), length, 0)
    while bit > least:
        lengths = lengths + swap(lengths, "page", bit)
        bit //= 2
    return lengths


ORDER = (
    ("first",),
    ("lengths",),
    ("pack",),
    ("spread",),
    ("second", 0),
    ("wide", 0),
    ("second", 1),
    ("join", 0),
    ("after_two", 0),
    ("join", 1),
    ("wide", 1),
    ("join", 2),
    ("join", 3),
    ("forward", 0),
    ("forward", 1),
    ("broad", "gate", 0),
    ("broad", "up", 0),
    ("finish", 0),
    ("forward", 2),
    ("finish", 1),
    ("after_last", 2),
    ("forward", 3),
    ("broad", "gate", 1),
    ("broad", "up", 1),
    ("finish", 2),
    ("finish", 3),
)


def packed_device(tile_tokens, page_lengths, occupancy, block_mix, stride_mix, w_gate_up, w_down):
    ids = jnp.stack([lax.axis_index("page"), lax.axis_index("tok")]).astype(jnp.int32)
    pages, parts = lax.axis_size("page"), lax.axis_size("tok")
    feat_width = tile_tokens.shape[2]
    spans = [feat_width * eighths // 8 for eighths in SPANS]
    tokens, held = [], {}

    def chained(name, step, *operands):
        results, token = step(*operands, (list(tokens), BRIEF))
        tokens[:] = [token]
        return results

    def plane(value):
        here = 2 * parts
        groups = [[level * here + i for i in range(here)] for level in range(pages // 2)]
        return lax.all_gather(value.reshape((-1,) + value.shape[2:]), AXES, axis_index_groups=groups)

    far_lengths = some_lengths(page_lengths[0], pages // 2, 1)
    lengths = far_lengths + swap(far_lengths, "page", 1)
    place = [ids, lengths]

    def swap_pages(k, own):
        held["own", k], held["got", k] = own, swap(own, "page", 1)

    def pack():
        value = chained("pack", pack_weights, jnp.swapaxes(w_gate_up, 1, 2), jnp.swapaxes(w_down, 0, 1))[0]
        held["weights"], held["across"] = value, swap(value, "page", 4)

    def first():
        groups = (spans[0], sum(spans[1:]))
        found = chained("first", first_factor, ids, page_lengths, occupancy, tile_tokens, block_mix, parts, groups)
        for k in range(2):
            mine = found[k * parts:(k + 1) * parts]
            held["first", k] = mine[:1] + [swap(mine[other], "tok", other) for other in range(1, parts)]

    def spread():
        held["spread"] = chained("spread", spread_stride, ids, stride_mix, parts)[0]

    def second(k):
        begin, here = (spans[0], spans[1:]) if k else (0, spans[:1])
        operands = (begin, here, *place, occupancy, held["spread"], held["first", k], tile_tokens)
        for i, own in enumerate(chained("second", second_factor, *operands)):
            swap_pages(k + i, own)

    def paired(value, got, which, place):
        return chained("wide", pair_up, ids, value, got, which, place)[0]

    def wide(k):
        value = paired(held["weights"], held["across"], (0, 4 - 2 * k), k)
        held["weights"] = value
        if k == 0:
            held["across"] = swap(value, "page", 2)
        else:
            value = value.reshape((-1,) + value.shape[2:])
            cut = value.shape[1] // 2
            held["gate"], held["up"] = value[:, :cut], value[:, cut:]
            held["gate_got"], held["up_got"] = swap(held["gate"], "tok", 2), swap(held["up"], "page", 1)

    def broad(kind, k):
        bits = ((1, 2), (0, 1))
        y_first = kind == "gate"
        which = bits[k] if y_first else bits[1 - k]
        value = paired(held[kind], held[kind + "_got"], which, 0 if y_first or k == 0 else 1)
        if k == 0:
            next_axis = ("page", 1) if y_first else ("tok", 2)
            held[kind], held[kind + "_got"] = value, swap(value, *next_axis)
        else:
            value = value.reshape((-1,) + value.shape[2:])
            held[kind], held[kind + "_got"] = value, swap(value, "tok", 1)

    def join(k):
        value = chained("join", join_parity, *place, held["own", k], held["got", k])[0]
        held["one", k] = lax.ppermute(value, "page", [(4, 2), (5, 3), (6, 4), (7, 5)])
        held["two", k] = lax.ppermute(value, "page", [(6, 2), (7, 3), (2, 6), (3, 7)])
        held["own", k] = value

    def forward(k):
        value = chained("forward", forward_merge, *place, held["own", k], held["one", k], held["two", k])[0]
        held["last", k] = lax.ppermute(value, "page", [(2, 0), (3, 1), (0, 2), (1, 3)])

    def finish(k):
        found = [held[kind, k] for kind in ("own", "one", "two", "last")]
        held["source", k] = chained("finish", final_merge, *place, *found)[0]

    def lengths_first():
        tokens.append(far_lengths)

    def after_one(k):
        tokens.append(held["one", k])

    def after_two(k):
        tokens.append(held["two", k])

    def after_last(k):
        tokens.append(held["last", k])

    steps = dict(pack=pack, first=first, spread=spread, second=second, wide=wide, broad=broad)
    steps.update(join=join, forward=forward, finish=finish, lengths=lengths_first)
    steps.update(after_one=after_one, after_two=after_two, after_last=after_last)
    for name, *which in ORDER:
        steps[name](*which)
    weights = [held[kind] for kind in ("gate", "gate_got", "up", "up_got")]
    return packed_mlp(ids, [held["source", k] for k in range(len(spans))], weights)


def solution(mesh):
    pages, parts = mesh.shape["page"], mesh.shape["tok"]
    return jax.shard_map(
        packed_device if (pages, parts) == (8, 4) else per_device,
        mesh=mesh,
        in_specs=(
            P("page", "tok", None),
            P("page"),
            P("page", "tok"),
            P("tok", None, None),
            P("tok", None, None),
            P(None, None, ("page", "tok")),
            P(None, ("page", "tok")),
        ),
        out_specs=P("tok", "page", None),
        check_vma=False,
    )
```
